256 devices in a mesh: context: 32 (over z, y_hi, core), expert: 8 (over x, y_lo).
Axes of the slice: x: 4, y: 4 (y_hi: 2, y_lo: 2; y = y_hi * 2 + y_lo), z: 8, core: 2. Of those that a mesh axis runs over, the one named last changes fastest.
Arguments:
- queries: bfloat16 [4096, 4096], P('context', 'expert'), may hold values from -150 to 150
- key_rows: bfloat16 [4096, 512], P('context'), may hold values from -6 to 6
- value_rows: bfloat16 [4096, 512], P('context'), may hold values from -6 to 6
- span_order: int32 [64], replicated, may hold values from 0 to 63, each once
- residual: bfloat16 [4096, 4096], P('context', 'expert'), may hold values from -40 to 40
- norm_gain: float32 [4096], replicated, may hold values from 0.1 to 1.9
- out_weight: bfloat16 [4096, 4096], P('expert', 'context'), may hold values from -0.09375 to 0.09375
- gate_weight: bfloat16 [64, 1536, 4096], P('context', 'expert'), may hold values from -0.09375 to 0.09375
- up_weight: bfloat16 [64, 1536, 4096], P('context', 'expert'), may hold values from -0.09375 to 0.09375
- down_weight: bfloat16 [64, 1536, 4096], P('context', 'expert'), may hold values from -0.15625 to 0.15625
- routes: int32 [4096, 8], P('context'), may hold values from 0 to 63, all different within a row; in each aligned block of 128 rows (0 to 127, 128 to 255, ...) at most 20 rows name the same one
- route_weights: float32 [4096, 8], P('context'), may hold values from 0.05 to 1
Outputs:
- attended: bfloat16 [4096, 4096], P('context', 'expert')
- layer_output: bfloat16 [4096, 4096], P('context', 'expert')
The draws below stay inside these ranges and needn't reach their ends.
Inputs may be any that keep to these rules, and one draw needn't show every extreme that they name: `span_order`: each span number appears once. `routes`: A token names 8 different experts; within the rows of one device (aligned blocks of 128 rows) no expert is named by more than 20 rows, a bound that some block reaches.
All inputs are finite; a program needn't handle non-finite values.
Results may differ from the reference program's by a relative error of at most 0.007.
Values may be sent and summed in bfloat16 or wider, within the bound.
No kernel may reach another device: no remote copies, remote signals or barrier semaphores. Data moves between devices by JAX's collectives and lax.ppermute only.
A program may use at most 128 MiB of HBM per device.

```python
import math
import jax
import jax.numpy as jnp
import numpy as np
from jax import lax

D = 4096
HD = 128
QH = 32
KVH = 4
HID = 1536
TOPK = 8
TOK_DEV = 128
TOKENS = 4096
SPAN = 64
NCHUNK = 64
GROUP = 8
HID_DEV = 192
EXPERTS = 64
CAP = 20
N_CONTEXT = 32
N_EXPERT = 8


def shared_keys(key):
    return jnp.clip(jax.random.normal(key, (TOKENS, KVH * HD), jnp.float32), -6.0, 6.0)


def draw_key_rows(key, part):
    base_draw = shared_keys(key)
    return base_draw.astype(jnp.bfloat16)


def draw_queries(key, part):
    key = jax.random.fold_in(key, 12)
    fresh_draw = jnp.clip(jax.random.normal(key, (TOKENS, QH * HD), jnp.float32), -6.0, 6.0)
    return fresh_draw.astype(jnp.bfloat16)


def draw_residual(key, part):
    key = jax.random.fold_in(key, 13)
    first_key = jax.random.fold_in(key, 0)
    column_ramp = 3.0 ** (0.5 * jnp.arange(D, dtype=jnp.float32) / D)
    normal_draw = jax.random.normal(first_key, (TOKENS, D), jnp.float32)
    return jnp.clip(normal_draw * column_ramp, -40.0, 40.0).astype(jnp.bfloat16)


def shard_levels(key, dims, shards, low, top_value):
    factor_of = 1.0
    for position, shards_of in shards:
        steps = jax.random.uniform(jax.random.fold_in(jax.random.fold_in(key, 6), position), (shards_of,), jnp.float32, low / len(shards), top_value / len(shards))
        factor_of = factor_of * jnp.repeat(jnp.exp(steps), dims[position] // shards_of).reshape((-1,) + (1,) * (len(dims) - 1 - position))
    return factor_of


def deal_out(key, own, number, rows, count, top, most, skew):
    order = jax.random.permutation(key, count)
    packed, usual = portions_of(count, rows * top, most, skew, True), portions_of(count, rows * top, most, skew, False)
    places = jnp.arange(count)

    def named(tallies, rotation):
        used = int((tallies > 0).sum())
        fixed = max(1, used // 4)
        shifted = fixed + (places - fixed + rotation * (used - fixed)) % max(1, count - fixed)
        return jnp.zeros((count,), jnp.int32).at[order[jnp.where(places < fixed, places, shifted)]].set(jnp.asarray(tallies, jnp.int32))

    tallies = jnp.where(number % 4 == 0, named(packed, number // 4), named(usual, number - number // 4 - 1))
    mixed = jax.random.permutation(jax.random.fold_in(own, 3), count)
    source_of, taker = mixed[0:count // 2 * 2:2], mixed[1:count // 2 * 2:2]
    margin = jnp.minimum(tallies[source_of] - 1, most - tallies[taker]) // 2
    margin = jnp.where((source_of == order[0]) | (taker == order[0]) | (tallies[taker] == 0), 0, jnp.maximum(margin, 0))
    shifted = jax.random.randint(jax.random.fold_in(own, 4), (count // 2,), 0, 1 << 20) % (margin + 1)
    tallies = tallies.at[source_of].add(-shifted).at[taker].add(shifted)
    items = jnp.searchsorted(jnp.cumsum(tallies), jnp.arange(rows * top), side="right").astype(jnp.int32)
    table = items.reshape(top, rows).T
    table = table[jax.random.permutation(jax.random.fold_in(own, 1), rows)]
    rotation = jax.random.randint(jax.random.fold_in(own, 2), (rows, 1), 0, top)
    return jnp.take_along_axis(table, (jnp.arange(top)[None, :] + rotation) % top, axis=1)


def portions_of(amount, total, reach, lean, full):
    loads = [(1 << 20) // math.isqrt(standing ** lean) + 1 for standing in range(1, amount + 1)]
    largest = reach if full else min(reach, max(-(-total // amount), total * loads[0] // sum(loads)))
    least = 1 if total - largest >= amount - 1 else 0
    holding, surplus = [largest] + [least] * (amount - 1), total - largest - least * (amount - 1)
    while surplus > 0:
        candidates = [i for i in range(1, amount) if holding[i] < largest] or [i for i in range(1, amount) if holding[i] < reach]
        pool, left = sum([loads[i] for i in candidates]), surplus
        for i in candidates:
            extra = min(reach - holding[i], max(1, left * loads[i] // pool), surplus)
            holding[i] = holding[i] + extra
            surplus = surplus - extra
    return np.array(holding)


def noise(key, extent, spread, bound, shards=(), held_as=jnp.bfloat16):
    factor_of = shard_levels(key, extent, shards, -0.22, 0.18) if shards else 1.0
    result = jax.random.normal(key, extent, jnp.float32) * spread * factor_of
    return jnp.minimum(jnp.maximum(result, -bound), bound).astype(held_as)


def setup_inputs(seed: int = 0) -> dict:
    key_list = jax.random.split(jax.random.key(seed), 13)
    queries = draw_queries(jax.random.fold_in(key_list[12], 71), 0)
    key_rows = draw_key_rows(jax.random.fold_in(key_list[12], 71), 0)
    value_rows = noise(key_list[2], (TOKENS, KVH * HD), 1.0, 6.0, ((0, 32),))
    span_order = jax.random.permutation(key_list[3], NCHUNK).astype(jnp.int32)
    residual = draw_residual(jax.random.fold_in(key_list[12], 71), 0)
    norm_gain = jnp.clip(1.0 + 0.18 * jax.random.normal(key_list[5], (D,), jnp.float32), 0.1, 1.9)
    out_weight = noise(key_list[6], (QH * HD, D), (QH * HD) ** -0.5, 0.09375, ((0, 8), (1, 32)))
    gate_weight = noise(key_list[7], (EXPERTS, HID, D), D ** -0.5, 0.09375, ((0, 32), (1, 8)))
    up_weight = noise(key_list[8], (EXPERTS, HID, D), D ** -0.5, 0.09375, ((0, 32), (1, 8)))
    down_weight = noise(key_list[9], (EXPERTS, HID, D), HID ** -0.5, 0.15625, ((0, 32), (1, 8)))
    routes_keys = jax.random.split(jax.random.fold_in(key_list[10], 1), TOKENS // TOK_DEV)
    routes_turns = jax.random.permutation(jax.random.fold_in(key_list[10], 3), TOKENS // TOK_DEV)
    routes = jax.vmap(lambda own, number: deal_out(jax.random.fold_in(key_list[10], 2), own, number, TOK_DEV, EXPERTS, TOPK, CAP, 1))(routes_keys, routes_turns).reshape((TOKENS, TOPK))
    route_weights = jnp.clip(jnp.exp(math.log(1.0) - 2.9957323 * jax.random.uniform(key_list[11], (TOKENS, TOPK), jnp.float32) ** shard_levels(key_list[11], (TOKENS, TOPK), ((0, 32),), -0.2, 0.2)), 0.05, 1.0)
    return {"queries": queries, "key_rows": key_rows, "value_rows": value_rows, "span_order": span_order, "residual": residual, "norm_gain": norm_gain, "out_weight": out_weight, "gate_weight": gate_weight, "up_weight": up_weight, "down_weight": down_weight, "routes": routes, "route_weights": route_weights}


masked_score = -1e+30
norm_epsilon = 1e-06

def attention(queries, key_rows, value_rows, positions):
    scale_factor = HD ** (-0.5)
    allowed = positions[None, :] <= positions[:, None]

    def one_head(head_id):
        group_id = head_id // GROUP
        query_head = lax.dynamic_slice_in_dim(queries, head_id * HD, HD, 1)
        key_head = lax.dynamic_slice_in_dim(key_rows, group_id * HD, HD, 1)
        value_head = lax.dynamic_slice_in_dim(value_rows, group_id * HD, HD, 1)
        scores = jnp.dot(query_head, key_head.T, preferred_element_type=jnp.float32) * scale_factor
        scores = jnp.where(allowed, scores, masked_score)
        row_top = lax.optimization_barrier(jnp.max(scores, axis=1, keepdims=True))
        exp_terms = jnp.where(allowed, jnp.exp(scores - row_top), 0.0)
        totals = lax.optimization_barrier(jnp.sum(exp_terms, axis=1, keepdims=True))
        probs = exp_terms.astype(jnp.bfloat16)
        weighted = jnp.dot(probs, value_head, preferred_element_type=jnp.float32)
        return (weighted / totals).astype(jnp.bfloat16)
    head_outs = lax.map(one_head, jnp.arange(QH, dtype=jnp.int32))
    return jnp.transpose(head_outs, (1, 0, 2)).reshape(TOKENS, QH * HD)

def mixture_of_experts(normed, gate_weight, up_weight, down_weight, routes, route_weights):
    expert_ids = jnp.arange(EXPERTS, dtype=jnp.int32)
    matches = routes[:, :, None] == expert_ids
    member = jnp.any(matches, axis=1).astype(jnp.int32).reshape(N_CONTEXT, TOK_DEV, EXPERTS)
    before = (jnp.cumsum(member, axis=1) - member).reshape(TOKENS, EXPERTS)
    slots = lax.optimization_barrier(jnp.sum(jnp.where(matches, before[:, None, :], 0), axis=2)).astype(jnp.int32)
    block_ids = (jnp.arange(TOKENS, dtype=jnp.int32) // TOK_DEV)[:, None]
    buffer_index = (block_ids * CAP + slots).astype(jnp.int32)
    shares = route_weights / lax.optimization_barrier(jnp.sum(route_weights, axis=1, keepdims=True))
    token_ids = jnp.broadcast_to(jnp.arange(TOKENS, dtype=jnp.int32)[:, None], (TOKENS, TOPK))
    source = jnp.full((EXPERTS, N_CONTEXT * CAP), TOKENS, jnp.int32).at[routes, buffer_index].set(token_ids)
    coefficient = jnp.zeros((EXPERTS, N_CONTEXT * CAP), jnp.float32).at[routes, buffer_index].set(shares)
    padded = jnp.concatenate([normed, jnp.zeros((1, D), jnp.bfloat16)], axis=0)

    def one_expert(accumulated, inputs):
        row_source, weight, gate_matrix, up_matrix, down_matrix = inputs
        expert_rows = padded[row_source]
        gate_terms = jnp.dot(expert_rows, gate_matrix.T, preferred_element_type=jnp.float32)
        up_terms = jnp.dot(expert_rows, up_matrix.T, preferred_element_type=jnp.float32)
        activated = (jax.nn.silu(gate_terms) * up_terms).astype(jnp.bfloat16)
        slice_acts = activated.astype(jnp.float32).reshape(-1, N_EXPERT, HID_DEV)
        slice_down = down_matrix.astype(jnp.float32).reshape(N_EXPERT, HID_DEV, D)
        slice_out = jnp.einsum('rsh,shd->srd', slice_acts, slice_down)
        rounded = lax.optimization_barrier(slice_out.astype(jnp.bfloat16))
        expert_out = lax.optimization_barrier(jnp.sum(rounded.astype(jnp.float32), axis=0))
        accumulated = accumulated.at[row_source].add(expert_out * weight[:, None])
        return (accumulated, None)
    initial = jnp.zeros((TOKENS + 1, D), jnp.float32)
    accumulated, _ = lax.scan(one_expert, initial, (source, coefficient, gate_weight, up_weight, down_weight))
    return accumulated[:TOKENS]

def reference(queries, key_rows, value_rows, span_order, residual, norm_gain, out_weight, gate_weight, up_weight, down_weight, routes, route_weights):
    row_ids = jnp.arange(TOKENS, dtype=jnp.int32)
    positions = (span_order[row_ids // SPAN] * SPAN + row_ids % SPAN).astype(jnp.int32)
    heads_out = attention(queries, key_rows, value_rows, positions)
    state = residual.astype(jnp.float32) + jnp.dot(heads_out, out_weight, preferred_element_type=jnp.float32)
    row_scale = lax.rsqrt(lax.optimization_barrier(jnp.mean(state * state, axis=1, keepdims=True)) + norm_epsilon)
    normed = (state * row_scale * norm_gain).astype(jnp.bfloat16)
    mixture = mixture_of_experts(normed, gate_weight, up_weight, down_weight, routes, route_weights)
    return (state.astype(jnp.bfloat16), (state + mixture).astype(jnp.bfloat16))
```

```python
import functools

import jax
import jax.numpy as jnp
from jax import lax
from jax.experimental import pallas as pl
from jax.experimental.pallas import tpu as pltpu
from jax.sharding import PartitionSpec as P

D = 4096
HD = 128
QH = 32
KVH = 4
TOPK = 8
EXPERTS = 64
CAP = 20
SPAN = 64
NZ, NY, NCORE, NX, NYL = 8, 2, 2, 4, 2
N_CONTEXT = NZ * NY * NCORE
N_EXPERT = NX * NYL
ROWS = N_CONTEXT * 2 * CAP
WIDTH = D // N_EXPERT
HID_DEV = 192
TOK = 128

masked_score = -1e30
norm_epsilon = 1e-06
AXES = ("context", "expert")
f32 = jnp.float32
bf16 = jnp.bfloat16

RING = (0, -1, 1, -2, 2, -3, 3, 4)
PIECES = ((0, 0), (1, 0), (-1, 0), (0, 1), (2, 0), (-1, 1), (1, 1), (2, 1))


def flat_index(z, yh, core, x, yl):
    context = ((z % NZ) * NY + yh % NY) * NCORE + core % NCORE
    return context * N_EXPERT + (x % NX) * NYL + yl % NYL


@functools.lru_cache(None)
def pairs(dz, dy, dc, dx, dl):
    out = []
    for z in range(NZ):
        for yh in range(NY):
            for core in range(NCORE):
                for x in range(NX):
                    for yl in range(NYL):
                        out.append(
                            (
                                flat_index(z, yh, core, x, yl),
                                flat_index(z + dz, yh + dy, core + dc, x + dx, yl + dl),
                            )
                        )
    return tuple(out)


def shift(value, dz=0, dy=0, dc=0, dx=0, dl=0):
    return lax.ppermute(value, AXES, pairs(dz, dy, dc, dx, dl))


def context_ring(share):
    start = jnp.stack([share, shift(share, dy=1)])
    up = down = start
    mine = [start]
    for _ in range(3):
        up, down = shift(up, dz=1), shift(down, dz=-1)
        mine += [up, down]
    mine.append(shift(up, dz=1))
    return mine + [shift(v, dc=1) for v in mine]


def expert_gather(v):
    xp = shift(v, dx=-1)
    xm = shift(v, dx=1)
    yy = shift(v, dl=1)
    x2 = shift(xp, dx=-1)
    xmy = shift(yy, dx=1)
    xpy = shift(xp, dl=1)
    third = v.shape[0] // 3 // 16 * 16
    last = jnp.concatenate(
        [
            shift(x2[:third], dl=1),
            shift(xmy[third : 2 * third], dx=1),
            shift(xpy[2 * third :], dx=-1),
        ],
        axis=0,
    )
    return [v, xp, xm, yy, x2, xmy, xpy, last]


def attention_kernel(q_ref, qpos_ref, kpos_ref, *refs):
    pieces, out_ref, scores = refs[:16], refs[16], refs[17]
    heads = q_ref.shape[1] // HD
    q = jnp.concatenate([q_ref[:, h * HD : (h + 1) * HD] for h in range(heads)], axis=0)
    qpos = qpos_ref[...]
    top = None
    for i in range(16):
        keys = pieces[i][:, :, :HD].reshape(2 * TOK, HD)
        s = lax.dot_general(q, keys, (((1,), (1,)), ((), ())), preferred_element_type=f32)
        s = jnp.where(kpos_ref[i : i + 1, :] <= qpos, s * (HD**-0.5), masked_score)
        scores[:, i * 256 : (i + 1) * 256] = s
        top = s if top is None else jnp.maximum(top, s)
    top = jnp.max(top, axis=1, keepdims=True)
    total = None
    acc = None
    for i in range(16):
        values = pieces[i][:, :, HD:].reshape(2 * TOK, HD)
        p = jnp.exp(scores[:, i * 256 : (i + 1) * 256] - top)
        total = p if total is None else total + p
        term = jnp.dot(p.astype(bf16), values, preferred_element_type=f32)
        acc = term if acc is None else acc + term
    out = (acc / jnp.sum(total, axis=1, keepdims=True)).astype(bf16)
    for h in range(heads):
        out_ref[:, h * HD : (h + 1) * HD] = out[h * TOK : (h + 1) * TOK]


def attention(queries, qpos, kpos, pieces):
    heads = queries.shape[1] // HD
    return pl.pallas_call(
        attention_kernel,
        out_shape=jax.ShapeDtypeStruct(queries.shape, bf16),
        in_specs=[pl.BlockSpec(memory_space=pltpu.VMEM)] * 19,
        out_specs=pl.BlockSpec(memory_space=pltpu.VMEM),
        scratch_shapes=[pltpu.VMEM((heads * TOK, N_CONTEXT * TOK), f32)],
        compiler_params=pltpu.CompilerParams(vmem_limit_bytes=32 << 20),
        cost_estimate=pl.CostEstimate(
            flops=4 * heads * TOK * N_CONTEXT * TOK * HD,
            bytes_accessed=3 << 20,
            transcendentals=heads * TOK * N_CONTEXT * TOK,
        ),
    )(queries, qpos, kpos, *pieces)


def project_kernel(place_ref, a_ref, *refs):
    weights, out_ref = refs[:16], refs[16]
    a = a_ref[...]
    for i in range(16):
        both = jnp.concatenate([weights[i][0], weights[i][1]], axis=1)
        r = jnp.dot(a, both, preferred_element_type=f32).astype(bf16)
        target = place_ref[i % 8]
        core = place_ref[8] if i < 8 else 1 - place_ref[8]
        yh = place_ref[9]
        for k in range(2):
            block = (yh if k == 0 else 1 - yh) * 2 + core
            out_ref[target, :, pl.ds(pl.multiple_of(block * 128, 128), 128)] = r[
                :, k * 128 : (k + 1) * 128
            ]


def project(place, heads_out, pieces):
    return pl.pallas_call(
        project_kernel,
        out_shape=jax.ShapeDtypeStruct((N_EXPERT, TOK, WIDTH), bf16),
        in_specs=[pl.BlockSpec(memory_space=pltpu.SMEM)]
        + [pl.BlockSpec(memory_space=pltpu.VMEM)] * 17,
        out_specs=pl.BlockSpec(memory_space=pltpu.VMEM),
        compiler_params=pltpu.CompilerParams(vmem_limit_bytes=24 << 20),
        cost_estimate=pl.CostEstimate(
            flops=2 * TOK * WIDTH * D, bytes_accessed=5 << 20, transcendentals=0
        ),
    )(place, heads_out, *pieces)


def second_expert(axis, shape, first_row, per_block):
    rows = lax.broadcasted_iota(jnp.int32, shape, axis) + first_row
    return rows % per_block >= CAP


def up_kernel(tile, source_ref, gate_ref, up_ref, *refs):
    pieces, out_ref = refs[:8], refs[8]
    contract = (((1,), (1,)), ((), ()))
    sums = [[None, None], [None, None]]
    for i in range(8):
        rows = pieces[i][...]
        columns = pl.ds(pl.multiple_of(source_ref[i] * WIDTH, WIDTH), WIDTH)
        for j, ref in enumerate((gate_ref, up_ref)):
            for x in range(2):
                term = lax.dot_general(
                    ref[x, :, columns], rows, contract, preferred_element_type=f32
                )
                sums[j][x] = term if i == 0 else sums[j][x] + term
    second = second_expert(1, (HID_DEV, tile), pl.program_id(0) * tile, 2 * CAP)
    gate = jnp.where(second, sums[0][1], sums[0][0])
    up = jnp.where(second, sums[1][1], sums[1][0])
    out_ref[...] = (gate / (1.0 + jnp.exp(-gate)) * up).astype(bf16)


def up_project(source, gate_weight, up_weight, pieces, tile=256):
    rows = pieces[0].shape[0]
    whole = pl.BlockSpec(gate_weight.shape, lambda r: (0, 0, 0))
    return pl.pallas_call(
        functools.partial(up_kernel, tile),
        out_shape=jax.ShapeDtypeStruct((HID_DEV, rows), bf16),
        grid=(rows // tile,),
        in_specs=[pl.BlockSpec(memory_space=pltpu.SMEM), whole, whole]
        + [pl.BlockSpec((tile, WIDTH), lambda r: (r, 0))] * 8,
        out_specs=pl.BlockSpec((HID_DEV, tile), lambda r: (0, r)),
        compiler_params=pltpu.CompilerParams(vmem_limit_bytes=40 << 20),
        cost_estimate=pl.CostEstimate(
            flops=8 * rows * D * HID_DEV, bytes_accessed=18 << 20, transcendentals=rows * HID_DEV
        ),
    )(source, gate_weight, up_weight, *pieces)


def down_kernel(tile, *refs):
    acts, weights, out_ref = refs[:8], refs[8:16], refs[16]
    contract = (((0,), (0,)), ((), ()))
    sums = [None, None]
    for i in range(8):
        act = acts[i][...]
        for x in range(2):
            term = lax.dot_general(act, weights[i][x], contract, preferred_element_type=f32)
            sums[x] = term if i == 0 else sums[x] + term
    second = second_expert(0, (tile, WIDTH), pl.program_id(0) * tile, 2 * CAP)
    out_ref[...] = jnp.where(second, sums[1], sums[0]).astype(bf16)


def down_project(acts, weights, tile=256):
    rows = acts[0].shape[1]
    return pl.pallas_call(
        functools.partial(down_kernel, tile),
        out_shape=jax.ShapeDtypeStruct((rows, WIDTH), bf16),
        grid=(rows // tile,),
        in_specs=[pl.BlockSpec((HID_DEV, tile), lambda r: (0, r))] * 8
        + [pl.BlockSpec((2, HID_DEV, WIDTH), lambda r: (0, 0, 0))] * 8,
        out_specs=pl.BlockSpec((tile, WIDTH), lambda r: (r, 0)),
        compiler_params=pltpu.CompilerParams(vmem_limit_bytes=32 << 20),
        cost_estimate=pl.CostEstimate(
            flops=4 * rows * N_EXPERT * HID_DEV * WIDTH,
            bytes_accessed=9 << 20,
            transcendentals=0,
        ),
    )(*acts, *weights)


def local(
    queries,
    key_rows,
    value_rows,
    span_order,
    residual,
    norm_gain,
    out_weight,
    gate_weight,
    up_weight,
    down_weight,
    routes,
    route_weights,
):
    context = lax.axis_index("context")
    expert = lax.axis_index("expert")
    z, yh, core = context // 4, (context // 2) % 2, context % 2
    x, yl = expert // 2, expert % 2

    column = (expert * (QH // N_EXPERT) // (QH // KVH)) * HD
    share = jnp.concatenate(
        [
            lax.dynamic_slice_in_dim(key_rows, column, HD, 1),
            lax.dynamic_slice_in_dim(value_rows, column, HD, 1),
        ],
        axis=1,
    )
    kv_pieces = context_ring(share)
    w_pieces = context_ring(out_weight)

    down_pieces = []
    for dx, dl in PIECES:
        target = ((x - dx) % NX) * NYL + (yl + dl) % NYL
        part = lax.dynamic_slice_in_dim(down_weight, target * WIDTH, WIDTH, 2)
        down_pieces.append(part if (dx, dl) == (0, 0) else shift(part, dx=-dx, dl=dl))

    steps = jnp.array(RING, jnp.int32)
    ring_z = (z + steps) % NZ
    both = jnp.arange(2, dtype=jnp.int32)
    owner = (
        (ring_z[None, :, None] * NY + (yh + both)[None, None, :] % NY) * NCORE
        + ((core + both) % NCORE)[:, None, None]
    ).reshape(N_CONTEXT)
    span_ids = owner[:, None] * 2 + both
    ids = jnp.arange(span_order.shape[0], dtype=jnp.int32)
    spans = jnp.sum(jnp.where(span_ids[:, :, None] == ids, span_order, 0), axis=2)
    inner = jnp.arange(SPAN, dtype=jnp.int32)
    kpos = (spans[:, :, None] * SPAN + inner).reshape(16, 256)
    pair = lax.dynamic_slice_in_dim(span_order, context * 2, 2)
    qpos = (pair[:, None] * SPAN + inner).reshape(TOK, 1)
    qpos = jnp.concatenate([qpos] * (queries.shape[1] // HD), axis=0)

    heads_out = attention(queries, qpos, kpos, kv_pieces)
    place = jnp.concatenate([ring_z, core[None], yh[None]]).astype(jnp.int32)
    terms = project(place, heads_out, w_pieces)
    parts = lax.all_to_all(terms, "expert", 0, 0, tiled=True)
    state = residual.astype(f32) + jnp.sum(parts.astype(f32), axis=0)

    squares = jnp.sum(state * state, axis=1)
    squares = lax.all_to_all(
        jnp.broadcast_to(squares[None], (N_EXPERT, TOK)), "expert", 0, 0, tiled=True
    )
    row_scale = lax.rsqrt(jnp.sum(squares, axis=0) / D + norm_epsilon)
    gain = lax.dynamic_slice_in_dim(norm_gain, expert * WIDTH, WIDTH)
    normed = (state * row_scale[:, None] * gain).astype(bf16)

    expert_ids = jnp.arange(EXPERTS, dtype=jnp.int32)
    matches = routes[:, :, None] == expert_ids
    member = jnp.any(matches, axis=1)
    shares = route_weights / jnp.sum(route_weights, axis=1, keepdims=True)
    share_of = jnp.sum(jnp.where(matches, shares[:, :, None], 0.0), axis=1)
    token_ids = jnp.arange(TOK, dtype=jnp.int32)
    earlier = (token_ids[None, :] < token_ids[:, None]).astype(bf16)
    before = jnp.dot(earlier, member.astype(bf16), preferred_element_type=f32)
    code = jnp.where(member, before, -1.0).astype(bf16)
    row_ids = jnp.arange(ROWS, dtype=jnp.int32)
    spread = (row_ids[:, None] // CAP == expert_ids).astype(bf16)
    slot_of = (row_ids % CAP).astype(f32)
    coded = lax.dot_general(
        spread, code, (((1,), (1,)), ((), ())), preferred_element_type=f32
    )
    taken = (coded == slot_of[:, None]).astype(bf16)
    coded_t = lax.dot_general(
        code, spread, (((1,), (1,)), ((), ())), preferred_element_type=f32
    )
    taken_t = coded_t == slot_of[None, :]

    def coefficient(part):
        spread_out = lax.dot_general(
            part, spread, (((1,), (1,)), ((), ())), preferred_element_type=f32
        )
        return jnp.where(taken_t, spread_out, 0.0).astype(bf16)

    share_high = share_of.astype(bf16)
    share_low = (share_of - share_high.astype(f32)).astype(bf16)
    weights_high, weights_low = coefficient(share_high), coefficient(share_low)

    send = jnp.dot(taken, normed, preferred_element_type=f32).astype(bf16)
    received = lax.all_to_all(send, "context", 0, 0, tiled=True)
    row_pieces = expert_gather(received)
    source = jnp.stack(
        [((x + dx) % NX) * NYL + (yl + dl) % NYL for dx, dl in PIECES]
    ).astype(jnp.int32)
    act = up_project(source, gate_weight, up_weight, row_pieces)
    act_pieces = expert_gather(act)
    out = down_project(act_pieces, down_pieces)
    returned = lax.all_to_all(out, "context", 0, 0, tiled=True)
    mixture = jnp.dot(weights_high, returned, preferred_element_type=f32) + jnp.dot(
        weights_low, returned, preferred_element_type=f32
    )
    return (state.astype(bf16), (state + mixture).astype(bf16))


def solution(mesh):
    return jax.shard_map(
        local,
        mesh=mesh,
        in_specs=(
            P("context", "expert"),
            P("context", None),
            P("context", None),
            P(),
            P("context", "expert"),
            P(),
            P("expert", "context"),
            P("context", "expert", None),
            P("context", "expert", None),
            P("context", "expert", None),
            P("context", None),
            P("context", None),
        ),
        out_specs=(P("context", "expert"), P("context", "expert")),
        check_vma=False,
    )
```

```python
import functools

import jax
import jax.numpy as jnp
from jax import lax
from jax.experimental import pallas as pl
from jax.experimental.pallas import tpu as pltpu
from jax.sharding import PartitionSpec as P

D = 4096
HD = 128
QH = 32
KVH = 4
TOPK = 8
EXPERTS = 64
CAP = 20
SPAN = 64
NZ, NY, NCORE, NX, NYL = 8, 2, 2, 4, 2
N_CONTEXT = NZ * NY * NCORE
N_EXPERT = NX * NYL
CHUNKS = ((0, 40),)
WIDTH = D // N_EXPERT
HID_DEV = 192
TOK = 128

masked_score = -1e30
norm_epsilon = 1e-06
AXES = ("context", "expert")
f32 = jnp.float32
bf16 = jnp.bfloat16

RING = (0, -1, 1, -2, 2, -3, 3, 4)
PIECES = ((0, 0), (1, 0), (-1, 0), (0, 1), (2, 0), (-1, 1), (1, 1), (2, 1))


def flat_index(z, yh, core, x, yl):
    context = ((z % NZ) * NY + yh % NY) * NCORE + core % NCORE
    return context * N_EXPERT + (x % NX) * NYL + yl % NYL


@functools.lru_cache(None)
def pairs(dz, dy, dc, dx, dl):
    out = []
    for z in range(NZ):
        for yh in range(NY):
            for core in range(NCORE):
                for x in range(NX):
                    for yl in range(NYL):
                        out.append(
                            (
                                flat_index(z, yh, core, x, yl),
                                flat_index(z + dz, yh + dy, core + dc, x + dx, yl + dl),
                            )
                        )
    return tuple(out)


def shift(value, dz=0, dy=0, dc=0, dx=0, dl=0):
    return lax.ppermute(value, AXES, pairs(dz, dy, dc, dx, dl))


def context_ring(start, beside):
    up = down = start
    mine, other, made = [start], [], []
    waiting = [start]
    for step in range(3):
        cores = [shift(v, dc=1) for v in waiting]
        up, down = shift(up, dz=1), shift(down, dz=-1)
        up, down, cores, more = lax.optimization_barrier(
            (up, down, cores, beside[step](mine, other))
        )
        mine += [up, down]
        other += cores
        made.append(more)
        waiting = [up, down]
    cores = [shift(v, dc=1) for v in waiting]
    ends = [shift(up[0], dz=1), shift(down[1], dz=-1)]
    ends, cores, more = lax.optimization_barrier((ends, cores, beside[3](mine, other)))
    made.append(more)
    other += cores + [shift(v, dc=1) for v in ends]
    return mine + ends + other, made


def pair_of(refs, i, rows):
    half, step = divmod(i, 8)
    refs = refs[9 * half : 9 * half + 9]
    if step < 7:
        return refs[step][0, rows], refs[step][1, rows]
    return refs[7][rows], refs[8][rows]


def thirds_kernel(*refs):
    for source, target in zip(refs[:3], refs[3:]):
        target[...] = source[...]


def thirds(*arrays):
    rows, columns = arrays[0].shape
    part = -(-rows // 3 // 16) * 16
    specs = [
        pl.BlockSpec((part, columns), functools.partial(lambda k, r: (k, 0), k)) for k in range(3)
    ]
    return pl.pallas_call(
        thirds_kernel,
        out_shape=(jax.ShapeDtypeStruct((part, columns), arrays[0].dtype),) * 3,
        grid=(1,),
        in_specs=specs,
        out_specs=(pl.BlockSpec((part, columns), lambda r: (0, 0)),) * 3,
        compiler_params=pltpu.CompilerParams(vmem_limit_bytes=24 << 20),
        cost_estimate=pl.CostEstimate(
            flops=0, bytes_accessed=2 * rows * columns * 2, transcendentals=0
        ),
    )(*arrays)


def expert_stages(v, consume):
    first = (shift(v, dx=-1), shift(v, dx=1), shift(v, dl=1))
    carry = consume([v], 0, None)
    (xp, xm, yy), carry = lax.optimization_barrier((first, carry))
    second = (shift(xp, dx=-1), shift(yy, dx=1), shift(xp, dl=1))
    carry = consume([xp, xm, yy], 1, carry)
    (x2, xmy, xpy), carry = lax.optimization_barrier((second, carry))
    cut = thirds(x2, xmy, xpy)
    last = (shift(cut[0], dl=1), shift(cut[1], dx=1), shift(cut[2], dx=-1))
    carry = consume([x2, xmy, xpy], 4, carry)
    last, carry = lax.optimization_barrier((last, carry))
    return consume([jnp.concatenate(last, axis=0)[: v.shape[0]]], 7, carry)


W_ROWS = slice(0, 512)
K_ROWS = slice(512, 640)
V_ROWS = slice(640, 768)


def attention_kernel(count, carried, final, q_ref, qpos_ref, kpos_ref, *refs):
    refs = list(refs)
    before = [refs.pop(0) for _ in range(3)] if carried else None
    pieces = [refs.pop(0) for _ in range(count)]
    scores = refs.pop()
    heads = q_ref.shape[1] // HD
    q = jnp.concatenate([q_ref[:, h * HD : (h + 1) * HD] for h in range(heads)], axis=0)
    qpos = qpos_ref[...]
    top = None

    def rows_of(i, rows):
        ref = pieces[i]
        if len(ref.shape) == 2:
            return ref[rows]
        return jnp.concatenate([ref[0, rows], ref[1, rows]], axis=0)

    spans = []
    at = 0
    for i in range(count):
        keys = rows_of(i, K_ROWS)
        span = slice(at, at + keys.shape[0])
        spans.append(span)
        at = span.stop
        s = lax.dot_general(q, keys, (((1,), (1,)), ((), ())), preferred_element_type=f32)
        s = jnp.where(kpos_ref[:, span] <= qpos, s * (HD**-0.5), masked_score)
        scores[:, span] = s
        m = jnp.maximum(s[:, :HD], s[:, HD:]) if s.shape[1] > HD else s
        top = m if top is None else jnp.maximum(top, m)
    top = jnp.max(top, axis=1, keepdims=True)
    if carried:
        top = jnp.maximum(top, before[0][:, :1])
    total = None
    acc = None
    for i, span in enumerate(spans):
        p = jnp.exp(scores[:, span] - top)
        t = p[:, :HD] + p[:, HD:] if p.shape[1] > HD else p
        total = t if total is None else total + t
        term = jnp.dot(p.astype(bf16), rows_of(i, V_ROWS), preferred_element_type=f32)
        acc = term if acc is None else acc + term
    if carried:
        factor = jnp.exp(before[0][:, :1] - top)
        total = total + before[1][...] * factor
        acc = acc + before[2][...] * factor
    if not final:
        refs[0][...] = jnp.broadcast_to(top, (heads * TOK, HD))
        refs[1][...] = total
        refs[2][...] = acc
        return
    out = (acc / jnp.sum(total, axis=1, keepdims=True)).astype(bf16)
    for h in range(heads):
        refs[0][:, h * HD : (h + 1) * HD] = out[h * TOK : (h + 1) * TOK]


def attention(queries, qpos, kpos, pieces, before, final):
    heads = queries.shape[1] // HD
    keys = kpos.shape[1]
    part = jax.ShapeDtypeStruct((heads * TOK, HD), f32)
    ins = (queries, qpos, kpos, *(before or ()), *pieces)
    return pl.pallas_call(
        functools.partial(attention_kernel, len(pieces), before is not None, final),
        out_shape=jax.ShapeDtypeStruct(queries.shape, bf16) if final else (part, part, part),
        in_specs=[pl.BlockSpec(memory_space=pltpu.VMEM)] * len(ins),
        out_specs=pl.BlockSpec(memory_space=pltpu.VMEM)
        if final
        else (pl.BlockSpec(memory_space=pltpu.VMEM),) * 3,
        scratch_shapes=[pltpu.VMEM((heads * TOK, keys), f32)],
        compiler_params=pltpu.CompilerParams(vmem_limit_bytes=20 << 20),
        cost_estimate=pl.CostEstimate(
            flops=4 * heads * TOK * keys * HD,
            bytes_accessed=3 << 20,
            transcendentals=heads * TOK * keys,
        ),
    )(*ins)


def project_kernel(place_ref, a_ref, *refs):
    weights, out_ref = refs[:18], refs[18]
    a = a_ref[...]
    for i in range(16):
        both = jnp.concatenate(pair_of(weights, i, W_ROWS), axis=1)
        r = jnp.dot(a, both, preferred_element_type=f32).astype(bf16)
        target = place_ref[i % 8]
        core = place_ref[8] if i < 8 else 1 - place_ref[8]
        yh = place_ref[9]
        for k in range(2):
            block = (yh if k == 0 else 1 - yh) * 2 + core
            out_ref[target, :, pl.ds(pl.multiple_of(block * 128, 128), 128)] = r[
                :, k * 128 : (k + 1) * 128
            ]


def project(place, heads_out, pieces):
    return pl.pallas_call(
        project_kernel,
        out_shape=jax.ShapeDtypeStruct((N_EXPERT, TOK, WIDTH), bf16),
        in_specs=[pl.BlockSpec(memory_space=pltpu.SMEM)]
        + [pl.BlockSpec(memory_space=pltpu.VMEM)] * 19,
        out_specs=pl.BlockSpec(memory_space=pltpu.VMEM),
        compiler_params=pltpu.CompilerParams(vmem_limit_bytes=20 << 20),
        cost_estimate=pl.CostEstimate(
            flops=2 * TOK * WIDTH * D, bytes_accessed=5 << 20, transcendentals=0
        ),
    )(place, heads_out, *pieces)


def feature_blocks_kernel(in_ref, out_ref):
    out_ref[...] = in_ref[...].reshape(2 * HID_DEV, WIDTH)


def feature_blocks(weight):
    return pl.pallas_call(
        feature_blocks_kernel,
        out_shape=jax.ShapeDtypeStruct((N_EXPERT * 2 * HID_DEV, WIDTH), bf16),
        grid=(N_EXPERT,),
        in_specs=[pl.BlockSpec((2, HID_DEV, WIDTH), lambda r: (0, 0, r))],
        out_specs=pl.BlockSpec((2 * HID_DEV, WIDTH), lambda r: (r, 0)),
        compiler_params=pltpu.CompilerParams(vmem_limit_bytes=16 << 20),
        cost_estimate=pl.CostEstimate(flops=0, bytes_accessed=6 << 20, transcendentals=0),
    )(weight)


def experts_in(chunk):
    return tuple(x for x in range(2) if chunk[0] < (x + 1) * CAP and chunk[1] > x * CAP)


def choose(chunk, axis, tile, values):
    if len(values) == 1:
        return values[0]
    rows = lax.broadcasted_iota(jnp.int32, values[0].shape, axis) + pl.program_id(0) * tile
    second = rows % (chunk[1] - chunk[0]) >= CAP - chunk[0]
    return jnp.where(second, values[1], values[0])


def up_kernel(chunk, tile, count, carried, final, source_ref, *refs):
    refs = list(refs)
    before = [refs.pop(0) for _ in range(2)] if carried else None
    pieces = [refs.pop(0) for _ in range(count)]
    sources = [refs.pop(0) for _ in range(2)]
    inverses = [refs.pop(0) for _ in range(count)]
    held, done = refs.pop(-2), refs.pop(-1)

    @pl.when(pl.program_id(0) == 0)
    def _():
        copies = []
        for i in range(count):
            columns = pl.ds(pl.multiple_of(source_ref[i] * WIDTH, WIDTH), WIDTH)
            for j in range(2):
                k = 2 * i + j
                copies.append(
                    pltpu.make_async_copy(
                        sources[j].at[:, :, columns], held.at[k], done.at[k]
                    )
                )
        for copy in copies:
            copy.start()
        for copy in copies:
            copy.wait()

    contract = (((1,), (1,)), ((), ()))
    experts = experts_in(chunk)
    total, squares = None, None
    for i in range(count):
        rows = pieces[i][...]
        weights = jnp.concatenate([held[2 * i + j, x] for j in range(2) for x in experts], axis=0)
        term = lax.dot_general(weights, rows, contract, preferred_element_type=f32)
        total = term if total is None else total + term
        plain = rows.astype(f32) * inverses[i][...]
        squares = plain * plain if squares is None else squares + plain * plain
    ones = jnp.ones((16, WIDTH), bf16)
    high = squares.astype(bf16)
    low = (squares - high.astype(f32)).astype(bf16)
    square = lax.dot_general(ones, high, contract, preferred_element_type=f32)
    square = square + lax.dot_general(ones, low, contract, preferred_element_type=f32)
    parts = [total[k * HID_DEV : (k + 1) * HID_DEV] for k in range(2 * len(experts))]
    gate = choose(chunk, 1, tile, parts[: len(experts)])
    up = choose(chunk, 1, tile, parts[len(experts) :])
    if carried:
        gate = gate + before[0][:HID_DEV]
        up = up + before[0][HID_DEV:]
        square = square + before[1][...]
    if not final:
        refs[0][:HID_DEV] = gate
        refs[0][HID_DEV:] = up
        refs[1][...] = square
        return
    scale = lax.rsqrt(square / D + norm_epsilon)[:1]
    gate, up = gate * scale, up * scale
    refs[0][...] = (gate / (1.0 + jnp.exp(-gate)) * up).astype(bf16)


def up_project(chunk, source, inverse, gate_weight, up_weight, pieces, before, final, tile=256):
    rows = pieces[0].shape[0]
    count = len(pieces)

    def gain(i):
        return pl.BlockSpec((1, WIDTH), lambda r, at: (0, at[i]))

    sums = [
        pl.BlockSpec((2 * HID_DEV, tile), lambda r, at: (0, r)),
        pl.BlockSpec((16, tile), lambda r, at: (0, r)),
    ]
    act = pl.BlockSpec((HID_DEV, tile), lambda r, at: (0, r))
    return pl.pallas_call(
        functools.partial(up_kernel, chunk, tile, count, before is not None, final),
        out_shape=jax.ShapeDtypeStruct((HID_DEV, rows), bf16)
        if final
        else (
            jax.ShapeDtypeStruct((2 * HID_DEV, rows), f32),
            jax.ShapeDtypeStruct((16, rows), f32),
        ),
        grid_spec=pltpu.PrefetchScalarGridSpec(
            num_scalar_prefetch=1,
            grid=(rows // tile,),
            in_specs=(sums if before is not None else [])
            + [pl.BlockSpec((tile, WIDTH), lambda r, at: (r, 0))] * count
            + [pl.BlockSpec(memory_space=pltpu.HBM)] * 2
            + [gain(i) for i in range(count)],
            out_specs=act if final else tuple(sums),
            scratch_shapes=[
                pltpu.VMEM((2 * count, 2, HID_DEV, WIDTH), bf16),
                pltpu.SemaphoreType.DMA((2 * count,)),
            ],
        ),
        compiler_params=pltpu.CompilerParams(vmem_limit_bytes=28 << 20),
        cost_estimate=pl.CostEstimate(
            flops=4 * len(experts_in(chunk)) * rows * count * WIDTH * HID_DEV,
            bytes_accessed=count * (2 << 20),
            transcendentals=rows * HID_DEV,
        ),
    )(
        source,
        *(before or ()),
        *pieces,
        gate_weight,
        up_weight,
        *([inverse] * count),
    )


def down_kernel(chunk, tile, count, carried, final, source_ref, *refs):
    refs = list(refs)
    before = refs.pop(0) if carried else None
    acts, weights, out_ref = refs[:count], refs[count : 2 * count], refs[2 * count]
    contract = (((0,), (0,)), ((), ()))
    act = jnp.concatenate([ref[...] for ref in acts], axis=0)
    outs = []
    for x in experts_in(chunk):
        weight = jnp.concatenate([ref[0, x] for ref in weights], axis=0)
        outs.append(lax.dot_general(act, weight, contract, preferred_element_type=f32))
    out = choose(chunk, 0, tile, outs)
    if carried:
        out = out + before[...]
    out_ref[...] = out.astype(out_ref.dtype)


def down_project(chunk, source, acts, weights, before, final, tile=256):
    rows = acts[0].shape[1]
    count = len(acts)
    out = pl.BlockSpec((tile, WIDTH), lambda r, at: (r, 0))

    def weight(i):
        return pl.BlockSpec((1, 2, HID_DEV, WIDTH), lambda r, at: (at[i], 0, 0, 0))

    return pl.pallas_call(
        functools.partial(down_kernel, chunk, tile, count, before is not None, final),
        out_shape=jax.ShapeDtypeStruct((rows, WIDTH), bf16 if final else f32),
        grid_spec=pltpu.PrefetchScalarGridSpec(
            num_scalar_prefetch=1,
            grid=(rows // tile,),
            in_specs=([out] if before is not None else [])
            + [pl.BlockSpec((HID_DEV, tile), lambda r, at: (0, r))] * count
            + [weight(i) for i in range(count)],
            out_specs=out,
        ),
        compiler_params=pltpu.CompilerParams(vmem_limit_bytes=20 << 20),
        cost_estimate=pl.CostEstimate(
            flops=2 * len(experts_in(chunk)) * rows * count * HID_DEV * WIDTH,
            bytes_accessed=count * (1 << 20) + (3 << 20),
            transcendentals=0,
        ),
    )(source, *([before] if before is not None else []), *acts, *([weights] * count))


def local(
    queries,
    key_rows,
    value_rows,
    span_order,
    residual,
    norm_gain,
    out_weight,
    gate_weight,
    up_weight,
    down_weight,
    routes,
    route_weights,
):
    context = lax.axis_index("context")
    expert = lax.axis_index("expert")
    z, yh, core = context // 4, (context // 2) % 2, context % 2
    x, yl = expert // 2, expert % 2

    column = (expert * (QH // N_EXPERT) // (QH // KVH)) * HD
    share = jnp.concatenate(
        [
            out_weight,
            lax.dynamic_slice_in_dim(key_rows, column, HD, 1),
            lax.dynamic_slice_in_dim(value_rows, column, HD, 1),
        ],
        axis=0,
    )
    steps = jnp.array(RING, jnp.int32)
    ring_z = (z + steps) % NZ
    both = jnp.arange(2, dtype=jnp.int32)
    owner = (
        (ring_z[None, :, None] * NY + (yh + both)[None, None, :] % NY) * NCORE
        + ((core + both) % NCORE)[:, None, None]
    ).reshape(N_CONTEXT)
    span_ids = owner[:, None] * 2 + both
    ids = jnp.arange(span_order.shape[0], dtype=jnp.int32)
    spans = jnp.sum(jnp.where(span_ids[:, :, None] == ids, span_order, 0), axis=2)
    inner = jnp.arange(SPAN, dtype=jnp.int32)
    kpos = (spans[:, :, None] * SPAN + inner).reshape(1, N_CONTEXT * TOK)
    pair = lax.dynamic_slice_in_dim(span_order, context * 2, 2)
    qpos = (pair[:, None] * SPAN + inner).reshape(TOK, 1)
    qpos = jnp.concatenate([qpos] * (queries.shape[1] // HD), axis=0)

    expert_ids = jnp.arange(EXPERTS, dtype=jnp.int32)
    matches = routes[:, :, None] == expert_ids
    member = jnp.any(matches, axis=1)
    shares = route_weights / jnp.sum(route_weights, axis=1, keepdims=True)
    share_of = jnp.sum(jnp.where(matches, shares[:, :, None], 0.0), axis=1)
    token_ids = jnp.arange(TOK, dtype=jnp.int32)
    earlier = (token_ids[None, :] < token_ids[:, None]).astype(bf16)
    before = jnp.dot(earlier, member.astype(bf16), preferred_element_type=f32)
    code = jnp.where(member, before, -1.0).astype(bf16)
    share_high = share_of.astype(bf16)
    share_low = (share_of - share_high.astype(f32)).astype(bf16)
    source = jnp.stack(
        [((x + dx) % NX) * NYL + (yl + dl) % NYL for dx, dl in PIECES]
    ).astype(jnp.int32)
    last = (((1,), (1,)), ((), ()))
    sends, returns = [], []
    for first, end in CHUNKS:
        per_block = end - first
        row_ids = jnp.arange(N_CONTEXT * per_block, dtype=jnp.int32)
        place_ids = first + row_ids % per_block
        row_expert = row_ids // per_block * 2 + place_ids // CAP
        spread = (row_expert[:, None] == expert_ids).astype(bf16)
        slot_of = (place_ids % CAP).astype(f32)
        coded = lax.dot_general(spread, code, last, preferred_element_type=f32)
        sends.append((coded == slot_of[:, None]).astype(bf16))
        coded = lax.dot_general(code, spread, last, preferred_element_type=f32)
        taken = coded == slot_of[None, :]
        returns.append(
            [
                jnp.where(
                    taken, lax.dot_general(part, spread, last, preferred_element_type=f32), 0.0
                ).astype(bf16)
                for part in (share_high, share_low)
            ]
        )


    def keys_of(table, which):
        cuts = [table[:, begin[i] : begin[i] + (256 if i % 9 < 7 else 128)] for i in which]
        return jnp.concatenate(cuts, axis=1)

    begin = [256 * i for i in range(8)] + [1920]
    begin = begin + [2048 + v for v in begin]
    sets = (
        (0, 1, 2, 3, 4, 9, 10, 11),
        (5, 6, 12, 13),
        (7, 8, 14, 15, 16, 17),
    )
    parts = []

    def attend(step):
        def run(mine, other):
            pieces = [(other if i > 8 else mine)[i % 9] for i in sets[step]]
            before = parts[-1] if parts else None
            part = attention(queries, qpos, keys_of(kpos, sets[step]), pieces, before, step == 2)
            parts.append(part)
            return part

        return run

    start = jnp.stack([share, shift(share, dy=1)])
    start, down_cut = lax.optimization_barrier((start, feature_blocks(down_weight)))
    down_all = lax.all_to_all(down_cut, "expert", 0, 0, tiled=True)
    ring_pieces, made = context_ring(
        start,
        [
            lambda mine, other: [],
            lambda mine, other: [sends, returns],
            attend(0),
            lambda mine, other: (attend(1)(mine, other), down_all),
        ],
    )
    sends, returns = made[1]
    parts[-1], down_all = made[3]
    down_all = down_all.reshape(N_EXPERT, 2, HID_DEV, WIDTH)
    heads_out = attend(2)(ring_pieces[:9], ring_pieces[9:])
    place = jnp.concatenate([ring_z, core[None], yh[None]]).astype(jnp.int32)
    terms = project(place, heads_out, ring_pieces)
    parts = lax.all_to_all(terms, "expert", 0, 0, tiled=True)
    state = residual.astype(f32) + jnp.sum(parts.astype(f32), axis=0)

    gain = lax.dynamic_slice_in_dim(norm_gain, expert * WIDTH, WIDTH)
    scaled = (state * gain).astype(bf16)
    inverse = (1.0 / norm_gain)[None]

    received = []
    for table in sends:
        rows = jnp.dot(table, scaled, preferred_element_type=f32).astype(bf16)
        if received:
            rows, received[-1] = lax.optimization_barrier((rows, received[-1]))
        received.append(lax.all_to_all(rows, "context", 0, 0, tiled=True))
    mixture = None
    for chunk, rows, weights in zip(CHUNKS, received, returns):

        def up(group, at, carry):
            to = at + len(group)
            return up_project(
                chunk, source[at:to], inverse, gate_weight, up_weight, group, carry, to == 8
            )

        def down(group, at, carry):
            to = at + len(group)
            return down_project(chunk, source[at:to], group, down_all, carry, to == 8)

        out = expert_stages(expert_stages(rows, up), down)
        returned = lax.all_to_all(out, "context", 0, 0, tiled=True)
        for part in weights:
            term = jnp.dot(part, returned, preferred_element_type=f32)
            mixture = term if mixture is None else mixture + term
    return (state.astype(bf16), (state + mixture).astype(bf16))


def solution(mesh):
    return jax.shard_map(
        local,
        mesh=mesh,
        in_specs=(
            P("context", "expert"),
            P("context", None),
            P("context", None),
            P(),
            P("context", "expert"),
            P(),
            P("expert", "context"),
            P("context", "expert", None),
            P("context", "expert", None),
            P("context", "expert", None),
            P("context", None),
            P("context", None),
        ),
        out_specs=(P("context", "expert"), P("context", "expert")),
        check_vma=False,
    )
```

```python
import functools

import jax
import jax.numpy as jnp
from jax import lax
from jax.experimental import pallas as pl
from jax.experimental.pallas import tpu as pltpu
from jax.sharding import PartitionSpec as P

D = 4096
HD = 128
QH = 32
KVH = 4
TOPK = 8
EXPERTS = 64
CAP = 20
SPAN = 64
NZ, NY, NCORE, NX, NYL = 8, 2, 2, 4, 2
N_CONTEXT = NZ * NY * NCORE
N_EXPERT = NX * NYL
CHUNKS = ((0, 40),)
WIDTH = D // N_EXPERT
HID_DEV = 192
TOK = 128

masked_score = -1e30
norm_epsilon = 1e-06
AXES = ("context", "expert")
f32 = jnp.float32
bf16 = jnp.bfloat16

RING = (0, -1, 1, -2, 2, -3, 3, 4)
PIECES = ((0, 0), (1, 0), (-1, 0), (0, 1), (2, 0), (-1, 1), (1, 1), (2, 1))


def flat_index(z, yh, core, x, yl):
    context = ((z % NZ) * NY + yh % NY) * NCORE + core % NCORE
    return context * N_EXPERT + (x % NX) * NYL + yl % NYL


@functools.lru_cache(None)
def pairs(dz, dy, dc, dx, dl):
    out = []
    for z in range(NZ):
        for yh in range(NY):
            for core in range(NCORE):
                for x in range(NX):
                    for yl in range(NYL):
                        out.append(
                            (
                                flat_index(z, yh, core, x, yl),
                                flat_index(z + dz, yh + dy, core + dc, x + dx, yl + dl),
                            )
                        )
    return tuple(out)


def shift(value, dz=0, dy=0, dc=0, dx=0, dl=0):
    return lax.ppermute(value, AXES, pairs(dz, dy, dc, dx, dl))


def context_ring(share, beside):
    start = jnp.stack([share, shift(share, dy=1)])
    up = down = start
    mine, other, made = [start], [], []
    waiting = [start]
    for step in range(3):
        cores = [shift(v, dc=1) for v in waiting]
        up, down = shift(up, dz=1), shift(down, dz=-1)
        up, down, cores, more = lax.optimization_barrier(
            (up, down, cores, beside[step](mine, other))
        )
        mine += [up, down]
        other += cores
        made.append(more)
        waiting = [up, down]
    cores = [shift(v, dc=1) for v in waiting]
    ends = [shift(up[0], dz=1), shift(down[1], dz=-1)]
    ends, cores, more = lax.optimization_barrier((ends, cores, beside[3](mine, other)))
    made.append(more)
    other += cores + [shift(v, dc=1) for v in ends]
    return mine + ends + other, made


def pair_of(refs, i, rows):
    half, step = divmod(i, 8)
    refs = refs[9 * half : 9 * half + 9]
    if step < 7:
        return refs[step][0, rows], refs[step][1, rows]
    return refs[7][rows], refs[8][rows]


def thirds_kernel(*refs):
    for source, target in zip(refs[:3], refs[3:]):
        target[...] = source[...]


def thirds(*arrays):
    rows, columns = arrays[0].shape
    part = -(-rows // 3 // 16) * 16
    specs = [
        pl.BlockSpec((part, columns), functools.partial(lambda k, r: (k, 0), k)) for k in range(3)
    ]
    return pl.pallas_call(
        thirds_kernel,
        out_shape=(jax.ShapeDtypeStruct((part, columns), arrays[0].dtype),) * 3,
        grid=(1,),
        in_specs=specs,
        out_specs=(pl.BlockSpec((part, columns), lambda r: (0, 0)),) * 3,
        compiler_params=pltpu.CompilerParams(vmem_limit_bytes=24 << 20),
        cost_estimate=pl.CostEstimate(
            flops=0, bytes_accessed=2 * rows * columns * 2, transcendentals=0
        ),
    )(*arrays)


def expert_stages(v, consume):
    first = (shift(v, dx=-1), shift(v, dx=1), shift(v, dl=1))
    carry = consume([v], 0, None)
    (xp, xm, yy), carry = lax.optimization_barrier((first, carry))
    second = (shift(xp, dx=-1), shift(yy, dx=1), shift(xp, dl=1))
    carry = consume([xp, xm, yy], 1, carry)
    (x2, xmy, xpy), carry = lax.optimization_barrier((second, carry))
    cut = thirds(x2, xmy, xpy)
    last = (shift(cut[0], dl=1), shift(cut[1], dx=1), shift(cut[2], dx=-1))
    carry = consume([x2, xmy, xpy], 4, carry)
    last, carry = lax.optimization_barrier((last, carry))
    return consume([jnp.concatenate(last, axis=0)[: v.shape[0]]], 7, carry)


W_ROWS = slice(0, 512)
K_ROWS = slice(512, 640)
V_ROWS = slice(640, 768)


def attention_kernel(count, carried, final, q_ref, qpos_ref, kpos_ref, *refs):
    refs = list(refs)
    before = [refs.pop(0) for _ in range(3)] if carried else None
    pieces = [refs.pop(0) for _ in range(count)]
    scores = refs.pop()
    heads = q_ref.shape[1] // HD
    q = jnp.concatenate([q_ref[:, h * HD : (h + 1) * HD] for h in range(heads)], axis=0)
    qpos = qpos_ref[...]
    top = None

    def rows_of(i, rows):
        ref = pieces[i]
        if len(ref.shape) == 2:
            return ref[rows]
        return jnp.concatenate([ref[0, rows], ref[1, rows]], axis=0)

    spans = []
    at = 0
    for i in range(count):
        keys = rows_of(i, K_ROWS)
        span = slice(at, at + keys.shape[0])
        spans.append(span)
        at = span.stop
        s = lax.dot_general(q, keys, (((1,), (1,)), ((), ())), preferred_element_type=f32)
        s = jnp.where(kpos_ref[:, span] <= qpos, s * (HD**-0.5), masked_score)
        scores[:, span] = s
        m = jnp.maximum(s[:, :HD], s[:, HD:]) if s.shape[1] > HD else s
        top = m if top is None else jnp.maximum(top, m)
    top = jnp.max(top, axis=1, keepdims=True)
    if carried:
        top = jnp.maximum(top, before[0][:, :1])
    total = None
    acc = None
    for i, span in enumerate(spans):
        p = jnp.exp(scores[:, span] - top)
        t = p[:, :HD] + p[:, HD:] if p.shape[1] > HD else p
        total = t if total is None else total + t
        term = jnp.dot(p.astype(bf16), rows_of(i, V_ROWS), preferred_element_type=f32)
        acc = term if acc is None else acc + term
    if carried:
        factor = jnp.exp(before[0][:, :1] - top)
        total = total + before[1][...] * factor
        acc = acc + before[2][...] * factor
    if not final:
        refs[0][...] = jnp.broadcast_to(top, (heads * TOK, HD))
        refs[1][...] = total
        refs[2][...] = acc
        return
    out = (acc / jnp.sum(total, axis=1, keepdims=True)).astype(bf16)
    for h in range(heads):
        refs[0][:, h * HD : (h + 1) * HD] = out[h * TOK : (h + 1) * TOK]


def attention(queries, qpos, kpos, pieces, before, final):
    heads = queries.shape[1] // HD
    keys = kpos.shape[1]
    part = jax.ShapeDtypeStruct((heads * TOK, HD), f32)
    ins = (queries, qpos, kpos, *(before or ()), *pieces)
    return pl.pallas_call(
        functools.partial(attention_kernel, len(pieces), before is not None, final),
        out_shape=jax.ShapeDtypeStruct(queries.shape, bf16) if final else (part, part, part),
        in_specs=[pl.BlockSpec(memory_space=pltpu.VMEM)] * len(ins),
        out_specs=pl.BlockSpec(memory_space=pltpu.VMEM)
        if final
        else (pl.BlockSpec(memory_space=pltpu.VMEM),) * 3,
        scratch_shapes=[pltpu.VMEM((heads * TOK, keys), f32)],
        compiler_params=pltpu.CompilerParams(vmem_limit_bytes=20 << 20),
        cost_estimate=pl.CostEstimate(
            flops=4 * heads * TOK * keys * HD,
            bytes_accessed=3 << 20,
            transcendentals=heads * TOK * keys,
        ),
    )(*ins)


def project_kernel(place_ref, a_ref, *refs):
    weights, out_ref = refs[:18], refs[18]
    a = a_ref[...]
    for i in range(16):
        both = jnp.concatenate(pair_of(weights, i, W_ROWS), axis=1)
        r = jnp.dot(a, both, preferred_element_type=f32).astype(bf16)
        target = place_ref[i % 8]
        core = place_ref[8] if i < 8 else 1 - place_ref[8]
        yh = place_ref[9]
        for k in range(2):
            block = (yh if k == 0 else 1 - yh) * 2 + core
            out_ref[target, :, pl.ds(pl.multiple_of(block * 128, 128), 128)] = r[
                :, k * 128 : (k + 1) * 128
            ]


def project(place, heads_out, pieces):
    return pl.pallas_call(
        project_kernel,
        out_shape=jax.ShapeDtypeStruct((N_EXPERT, TOK, WIDTH), bf16),
        in_specs=[pl.BlockSpec(memory_space=pltpu.SMEM)]
        + [pl.BlockSpec(memory_space=pltpu.VMEM)] * 19,
        out_specs=pl.BlockSpec(memory_space=pltpu.VMEM),
        compiler_params=pltpu.CompilerParams(vmem_limit_bytes=20 << 20),
        cost_estimate=pl.CostEstimate(
            flops=2 * TOK * WIDTH * D, bytes_accessed=5 << 20, transcendentals=0
        ),
    )(place, heads_out, *pieces)


def experts_in(chunk):
    return tuple(x for x in range(2) if chunk[0] < (x + 1) * CAP and chunk[1] > x * CAP)


def choose(chunk, axis, tile, values):
    if len(values) == 1:
        return values[0]
    rows = lax.broadcasted_iota(jnp.int32, values[0].shape, axis) + pl.program_id(0) * tile
    second = rows % (chunk[1] - chunk[0]) >= CAP - chunk[0]
    return jnp.where(second, values[1], values[0])


def up_kernel(chunk, tile, count, carried, final, source_ref, *refs):
    refs = list(refs)
    before = [refs.pop(0) for _ in range(2)] if carried else None
    pieces = [refs.pop(0) for _ in range(count)]
    gates = [refs.pop(0) for _ in range(count)]
    ups = [refs.pop(0) for _ in range(count)]
    inverses = [refs.pop(0) for _ in range(count)]
    contract = (((1,), (1,)), ((), ()))
    experts = experts_in(chunk)
    total, squares = None, None
    for i in range(count):
        rows = pieces[i][...]
        weights = jnp.concatenate([ref[x] for ref in (gates[i], ups[i]) for x in experts], axis=0)
        term = lax.dot_general(weights, rows, contract, preferred_element_type=f32)
        total = term if total is None else total + term
        plain = rows.astype(f32) * inverses[i][...]
        squares = plain * plain if squares is None else squares + plain * plain
    ones = jnp.ones((16, WIDTH), bf16)
    high = squares.astype(bf16)
    low = (squares - high.astype(f32)).astype(bf16)
    square = lax.dot_general(ones, high, contract, preferred_element_type=f32)
    square = square + lax.dot_general(ones, low, contract, preferred_element_type=f32)
    parts = [total[k * HID_DEV : (k + 1) * HID_DEV] for k in range(2 * len(experts))]
    gate = choose(chunk, 1, tile, parts[: len(experts)])
    up = choose(chunk, 1, tile, parts[len(experts) :])
    if carried:
        gate = gate + before[0][:HID_DEV]
        up = up + before[0][HID_DEV:]
        square = square + before[1][...]
    if not final:
        refs[0][:HID_DEV] = gate
        refs[0][HID_DEV:] = up
        refs[1][...] = square
        return
    scale = lax.rsqrt(square / D + norm_epsilon)[:1]
    gate, up = gate * scale, up * scale
    refs[0][...] = (gate / (1.0 + jnp.exp(-gate)) * up).astype(bf16)


def up_project(chunk, source, inverse, gate_weight, up_weight, pieces, before, final, tile=256):
    rows = pieces[0].shape[0]
    count = len(pieces)

    def weight(i):
        return pl.BlockSpec((2, HID_DEV, WIDTH), lambda r, at: (0, 0, at[i]))

    def gain(i):
        return pl.BlockSpec((1, WIDTH), lambda r, at: (0, at[i]))

    sums = [
        pl.BlockSpec((2 * HID_DEV, tile), lambda r, at: (0, r)),
        pl.BlockSpec((16, tile), lambda r, at: (0, r)),
    ]
    act = pl.BlockSpec((HID_DEV, tile), lambda r, at: (0, r))
    return pl.pallas_call(
        functools.partial(up_kernel, chunk, tile, count, before is not None, final),
        out_shape=jax.ShapeDtypeStruct((HID_DEV, rows), bf16)
        if final
        else (
            jax.ShapeDtypeStruct((2 * HID_DEV, rows), f32),
            jax.ShapeDtypeStruct((16, rows), f32),
        ),
        grid_spec=pltpu.PrefetchScalarGridSpec(
            num_scalar_prefetch=1,
            grid=(rows // tile,),
            in_specs=(sums if before is not None else [])
            + [pl.BlockSpec((tile, WIDTH), lambda r, at: (r, 0))] * count
            + [weight(i) for i in range(count)] * 2
            + [gain(i) for i in range(count)],
            out_specs=act if final else tuple(sums),
        ),
        compiler_params=pltpu.CompilerParams(vmem_limit_bytes=28 << 20),
        cost_estimate=pl.CostEstimate(
            flops=4 * len(experts_in(chunk)) * rows * count * WIDTH * HID_DEV,
            bytes_accessed=count * (2 << 20),
            transcendentals=rows * HID_DEV,
        ),
    )(
        source,
        *(before or ()),
        *pieces,
        *([gate_weight] * count),
        *([up_weight] * count),
        *([inverse] * count),
    )


def down_kernel(chunk, tile, count, carried, final, *refs):
    refs = list(refs)
    before = refs.pop(0) if carried else None
    acts, weights, out_ref = refs[:count], refs[count : 2 * count], refs[2 * count]
    contract = (((0,), (0,)), ((), ()))
    act = jnp.concatenate([ref[...] for ref in acts], axis=0)
    outs = []
    for x in experts_in(chunk):
        weight = jnp.concatenate([ref[x] for ref in weights], axis=0)
        outs.append(lax.dot_general(act, weight, contract, preferred_element_type=f32))
    out = choose(chunk, 0, tile, outs)
    if carried:
        out = out + before[...]
    out_ref[...] = out.astype(out_ref.dtype)


def down_project(chunk, acts, weights, before, final, tile=256):
    rows = acts[0].shape[1]
    count = len(acts)
    out = pl.BlockSpec((tile, WIDTH), lambda r: (r, 0))
    return pl.pallas_call(
        functools.partial(down_kernel, chunk, tile, count, before is not None, final),
        out_shape=jax.ShapeDtypeStruct((rows, WIDTH), bf16 if final else f32),
        grid=(rows // tile,),
        in_specs=([out] if before is not None else [])
        + [pl.BlockSpec((HID_DEV, tile), lambda r: (0, r))] * count
        + [pl.BlockSpec((2, HID_DEV, WIDTH), lambda r: (0, 0, 0))] * count,
        out_specs=out,
        compiler_params=pltpu.CompilerParams(vmem_limit_bytes=20 << 20),
        cost_estimate=pl.CostEstimate(
            flops=2 * len(experts_in(chunk)) * rows * count * HID_DEV * WIDTH,
            bytes_accessed=count * (1 << 20) + (3 << 20),
            transcendentals=0,
        ),
    )(*([before] if before is not None else []), *acts, *weights)


def local(
    queries,
    key_rows,
    value_rows,
    span_order,
    residual,
    norm_gain,
    out_weight,
    gate_weight,
    up_weight,
    down_weight,
    routes,
    route_weights,
):
    context = lax.axis_index("context")
    expert = lax.axis_index("expert")
    z, yh, core = context // 4, (context // 2) % 2, context % 2
    x, yl = expert // 2, expert % 2

    column = (expert * (QH // N_EXPERT) // (QH // KVH)) * HD
    share = jnp.concatenate(
        [
            out_weight,
            lax.dynamic_slice_in_dim(key_rows, column, HD, 1),
            lax.dynamic_slice_in_dim(value_rows, column, HD, 1),
        ],
        axis=0,
    )
    steps = jnp.array(RING, jnp.int32)
    ring_z = (z + steps) % NZ
    both = jnp.arange(2, dtype=jnp.int32)
    owner = (
        (ring_z[None, :, None] * NY + (yh + both)[None, None, :] % NY) * NCORE
        + ((core + both) % NCORE)[:, None, None]
    ).reshape(N_CONTEXT)
    span_ids = owner[:, None] * 2 + both
    ids = jnp.arange(span_order.shape[0], dtype=jnp.int32)
    spans = jnp.sum(jnp.where(span_ids[:, :, None] == ids, span_order, 0), axis=2)
    inner = jnp.arange(SPAN, dtype=jnp.int32)
    kpos = (spans[:, :, None] * SPAN + inner).reshape(1, N_CONTEXT * TOK)
    pair = lax.dynamic_slice_in_dim(span_order, context * 2, 2)
    qpos = (pair[:, None] * SPAN + inner).reshape(TOK, 1)
    qpos = jnp.concatenate([qpos] * (queries.shape[1] // HD), axis=0)

    expert_ids = jnp.arange(EXPERTS, dtype=jnp.int32)
    matches = routes[:, :, None] == expert_ids
    member = jnp.any(matches, axis=1)
    shares = route_weights / jnp.sum(route_weights, axis=1, keepdims=True)
    share_of = jnp.sum(jnp.where(matches, shares[:, :, None], 0.0), axis=1)
    token_ids = jnp.arange(TOK, dtype=jnp.int32)
    earlier = (token_ids[None, :] < token_ids[:, None]).astype(bf16)
    before = jnp.dot(earlier, member.astype(bf16), preferred_element_type=f32)
    code = jnp.where(member, before, -1.0).astype(bf16)
    share_high = share_of.astype(bf16)
    share_low = (share_of - share_high.astype(f32)).astype(bf16)
    source = jnp.stack(
        [((x + dx) % NX) * NYL + (yl + dl) % NYL for dx, dl in PIECES]
    ).astype(jnp.int32)
    last = (((1,), (1,)), ((), ()))
    sends, returns = [], []
    for first, end in CHUNKS:
        per_block = end - first
        row_ids = jnp.arange(N_CONTEXT * per_block, dtype=jnp.int32)
        place_ids = first + row_ids % per_block
        row_expert = row_ids // per_block * 2 + place_ids // CAP
        spread = (row_expert[:, None] == expert_ids).astype(bf16)
        slot_of = (place_ids % CAP).astype(f32)
        coded = lax.dot_general(spread, code, last, preferred_element_type=f32)
        sends.append((coded == slot_of[:, None]).astype(bf16))
        coded = lax.dot_general(code, spread, last, preferred_element_type=f32)
        taken = coded == slot_of[None, :]
        returns.append(
            [
                jnp.where(
                    taken, lax.dot_general(part, spread, last, preferred_element_type=f32), 0.0
                ).astype(bf16)
                for part in (share_high, share_low)
            ]
        )


    down_cuts = []
    for dx, dl in PIECES:
        target = ((x - dx) % NX) * NYL + (yl + dl) % NYL
        down_cuts.append(lax.dynamic_slice_in_dim(down_weight, target * WIDTH, WIDTH, 2))

    def keys_of(table, which):
        cuts = [table[:, begin[i] : begin[i] + (256 if i % 9 < 7 else 128)] for i in which]
        return jnp.concatenate(cuts, axis=1)

    begin = [256 * i for i in range(8)] + [1920]
    begin = begin + [2048 + v for v in begin]
    sets = (
        (0, 1, 2, 3, 4, 9, 10, 11),
        (5, 6, 12, 13),
        (7, 8, 14, 15, 16, 17),
    )
    parts = []

    def attend(step):
        def run(mine, other):
            pieces = [(other if i > 8 else mine)[i % 9] for i in sets[step]]
            before = parts[-1] if parts else None
            part = attention(queries, qpos, keys_of(kpos, sets[step]), pieces, before, step == 2)
            parts.append(part)
            return part

        return run

    def down_from(i):
        return shift(down_cuts[i], dx=-PIECES[i][0])

    def relayed(i):
        return shift(down_cuts[i], dl=1)

    ring_pieces, made = context_ring(
        share,
        [
            lambda mine, other: [down_from(1), relayed(3), down_cuts],
            lambda mine, other: [down_from(2), relayed(5), sends, returns],
            lambda mine, other: [down_from(4), relayed(6), attend(0)(mine, other)],
            lambda mine, other: [relayed(7), attend(1)(mine, other)],
        ],
    )
    xp_down, y_down, down_cuts = made[0]
    xm_down, xmy_down, sends, returns = made[1]
    two_down, xpy_down, _ = made[2]
    far_down, parts[-1] = made[3]
    heads_out = attend(2)(ring_pieces[:9], ring_pieces[9:])
    place = jnp.concatenate([ring_z, core[None], yh[None]]).astype(jnp.int32)
    terms = project(place, heads_out, ring_pieces)
    parts = lax.all_to_all(terms, "expert", 0, 0, tiled=True)
    state = residual.astype(f32) + jnp.sum(parts.astype(f32), axis=0)

    gain = lax.dynamic_slice_in_dim(norm_gain, expert * WIDTH, WIDTH)
    scaled = (state * gain).astype(bf16)
    inverse = (1.0 / norm_gain)[None]

    received = []
    for table in sends:
        rows = jnp.dot(table, scaled, preferred_element_type=f32).astype(bf16)
        if received:
            rows, received[-1] = lax.optimization_barrier((rows, received[-1]))
        received.append(lax.all_to_all(rows, "context", 0, 0, tiled=True))
    down_pieces = [down_cuts[0], xp_down, xm_down, y_down, two_down]
    down_pieces += [
        shift(xmy_down, dx=1),
        shift(xpy_down, dx=-1),
        shift(far_down, dx=2),
    ]
    received[0], down_pieces = lax.optimization_barrier((received[0], down_pieces))
    mixture = None
    for chunk, rows, weights in zip(CHUNKS, received, returns):

        def up(group, at, carry):
            to = at + len(group)
            return up_project(
                chunk, source[at:to], inverse, gate_weight, up_weight, group, carry, to == 8
            )

        def down(group, at, carry):
            to = at + len(group)
            return down_project(chunk, group, down_pieces[at:to], carry, to == 8)

        out = expert_stages(expert_stages(rows, up), down)
        returned = lax.all_to_all(out, "context", 0, 0, tiled=True)
        for part in weights:
            term = jnp.dot(part, returned, preferred_element_type=f32)
            mixture = term if mixture is None else mixture + term
    return (state.astype(bf16), (state + mixture).astype(bf16))


def solution(mesh):
    return jax.shard_map(
        local,
        mesh=mesh,
        in_specs=(
            P("context", "expert"),
            P("context", None),
            P("context", None),
            P(),
            P("context", "expert"),
            P(),
            P("expert", "context"),
            P("context", "expert", None),
            P("context", "expert", None),
            P("context", "expert", None),
            P("context", None),
            P("context", None),
        ),
        out_specs=(P("context", "expert"), P("context", "expert")),
        check_vma=False,
    )
```

```python
import functools

import jax
import jax.numpy as jnp
from jax import lax
from jax.experimental import pallas as pl
from jax.experimental.pallas import tpu as pltpu
from jax.sharding import PartitionSpec as P

D = 4096
HD = 128
QH = 32
KVH = 4
TOPK = 8
EXPERTS = 64
CAP = 20
SPAN = 64
NZ, NY, NCORE, NX, NYL = 8, 2, 2, 4, 2
N_CONTEXT = NZ * NY * NCORE
N_EXPERT = NX * NYL
CHUNKS = ((0, 40),)
WIDTH = D // N_EXPERT
HID_DEV = 192
TOK = 128

masked_score = -1e30
norm_epsilon = 1e-06
AXES = ("context", "expert")
f32 = jnp.float32
bf16 = jnp.bfloat16

RING = (0, -1, 1, -2, 2, -3, 3, 4)
PIECES = ((0, 0), (1, 0), (-1, 0), (0, 1), (2, 0), (-1, 1), (1, 1), (2, 1))


def flat_index(z, yh, core, x, yl):
    context = ((z % NZ) * NY + yh % NY) * NCORE + core % NCORE
    return context * N_EXPERT + (x % NX) * NYL + yl % NYL


@functools.lru_cache(None)
def pairs(dz, dy, dc, dx, dl):
    out = []
    for z in range(NZ):
        for yh in range(NY):
            for core in range(NCORE):
                for x in range(NX):
                    for yl in range(NYL):
                        out.append(
                            (
                                flat_index(z, yh, core, x, yl),
                                flat_index(z + dz, yh + dy, core + dc, x + dx, yl + dl),
                            )
                        )
    return tuple(out)


def shift(value, dz=0, dy=0, dc=0, dx=0, dl=0):
    return lax.ppermute(value, AXES, pairs(dz, dy, dc, dx, dl))


def context_ring(start, beside):
    up = down = start
    mine, other, made = [start], [], []
    waiting = [start]
    for step in range(3):
        cores = [shift(v, dc=1) for v in waiting]
        up, down = shift(up, dz=1), shift(down, dz=-1)
        up, down, cores, more = lax.optimization_barrier(
            (up, down, cores, beside[step](mine, other))
        )
        mine += [up, down]
        other += cores
        made.append(more)
        waiting = [up, down]
    cores = [shift(v, dc=1) for v in waiting]
    ends = [shift(up[0], dz=1), shift(down[1], dz=-1)]
    ends, cores, more = lax.optimization_barrier((ends, cores, beside[3](mine, other)))
    made.append(more)
    other += cores + [shift(v, dc=1) for v in ends]
    return mine + ends + other, made


def pair_of(refs, i, rows):
    half, step = divmod(i, 8)
    refs = refs[9 * half : 9 * half + 9]
    if step < 7:
        return refs[step][0, rows], refs[step][1, rows]
    return refs[7][rows], refs[8][rows]


def thirds_kernel(*refs):
    for source, target in zip(refs[:3], refs[3:]):
        target[...] = source[...]


def thirds(*arrays):
    rows, columns = arrays[0].shape
    part = -(-rows // 3 // 16) * 16
    specs = [
        pl.BlockSpec((part, columns), functools.partial(lambda k, r: (k, 0), k)) for k in range(3)
    ]
    return pl.pallas_call(
        thirds_kernel,
        out_shape=(jax.ShapeDtypeStruct((part, columns), arrays[0].dtype),) * 3,
        grid=(1,),
        in_specs=specs,
        out_specs=(pl.BlockSpec((part, columns), lambda r: (0, 0)),) * 3,
        compiler_params=pltpu.CompilerParams(vmem_limit_bytes=24 << 20),
        cost_estimate=pl.CostEstimate(
            flops=0, bytes_accessed=2 * rows * columns * 2, transcendentals=0
        ),
    )(*arrays)


def expert_stages(v, consume):
    first = (shift(v, dx=-1), shift(v, dx=1), shift(v, dl=1))
    carry = consume([v], 0, None)
    (xp, xm, yy), carry = lax.optimization_barrier((first, carry))
    second = (shift(xp, dx=-1), shift(yy, dx=1), shift(xp, dl=1))
    carry = consume([xp, xm, yy], 1, carry)
    (x2, xmy, xpy), carry = lax.optimization_barrier((second, carry))
    cut = thirds(x2, xmy, xpy)
    last = (shift(cut[0], dl=1), shift(cut[1], dx=1), shift(cut[2], dx=-1))
    carry = consume([x2, xmy, xpy], 4, carry)
    last, carry = lax.optimization_barrier((last, carry))
    return consume([jnp.concatenate(last, axis=0)[: v.shape[0]]], 7, carry)


W_ROWS = slice(0, 512)
K_ROWS = slice(512, 640)
V_ROWS = slice(640, 768)


def attention_kernel(count, carried, final, q_ref, qpos_ref, kpos_ref, *refs):
    refs = list(refs)
    before = [refs.pop(0) for _ in range(3)] if carried else None
    pieces = [refs.pop(0) for _ in range(count)]
    scores = refs.pop()
    heads = q_ref.shape[1] // HD
    q = jnp.concatenate([q_ref[:, h * HD : (h + 1) * HD] for h in range(heads)], axis=0)
    qpos = qpos_ref[...]
    top = None

    def rows_of(i, rows):
        ref = pieces[i]
        if len(ref.shape) == 2:
            return ref[rows]
        return jnp.concatenate([ref[0, rows], ref[1, rows]], axis=0)

    spans = []
    at = 0
    for i in range(count):
        keys = rows_of(i, K_ROWS)
        span = slice(at, at + keys.shape[0])
        spans.append(span)
        at = span.stop
        s = lax.dot_general(q, keys, (((1,), (1,)), ((), ())), preferred_element_type=f32)
        s = jnp.where(kpos_ref[:, span] <= qpos, s * (HD**-0.5), masked_score)
        scores[:, span] = s
        m = jnp.maximum(s[:, :HD], s[:, HD:]) if s.shape[1] > HD else s
        top = m if top is None else jnp.maximum(top, m)
    top = jnp.max(top, axis=1, keepdims=True)
    if carried:
        top = jnp.maximum(top, before[0][:, :1])
    total = None
    acc = None
    for i, span in enumerate(spans):
        p = jnp.exp(scores[:, span] - top)
        t = p[:, :HD] + p[:, HD:] if p.shape[1] > HD else p
        total = t if total is None else total + t
        term = jnp.dot(p.astype(bf16), rows_of(i, V_ROWS), preferred_element_type=f32)
        acc = term if acc is None else acc + term
    if carried:
        factor = jnp.exp(before[0][:, :1] - top)
        total = total + before[1][...] * factor
        acc = acc + before[2][...] * factor
    if not final:
        refs[0][...] = jnp.broadcast_to(top, (heads * TOK, HD))
        refs[1][...] = total
        refs[2][...] = acc
        return
    out = (acc / jnp.sum(total, axis=1, keepdims=True)).astype(bf16)
    for h in range(heads):
        refs[0][:, h * HD : (h + 1) * HD] = out[h * TOK : (h + 1) * TOK]


def attention(queries, qpos, kpos, pieces, before, final):
    heads = queries.shape[1] // HD
    keys = kpos.shape[1]
    part = jax.ShapeDtypeStruct((heads * TOK, HD), f32)
    ins = (queries, qpos, kpos, *(before or ()), *pieces)
    return pl.pallas_call(
        functools.partial(attention_kernel, len(pieces), before is not None, final),
        out_shape=jax.ShapeDtypeStruct(queries.shape, bf16) if final else (part, part, part),
        in_specs=[pl.BlockSpec(memory_space=pltpu.VMEM)] * len(ins),
        out_specs=pl.BlockSpec(memory_space=pltpu.VMEM)
        if final
        else (pl.BlockSpec(memory_space=pltpu.VMEM),) * 3,
        scratch_shapes=[pltpu.VMEM((heads * TOK, keys), f32)],
        compiler_params=pltpu.CompilerParams(vmem_limit_bytes=20 << 20),
        cost_estimate=pl.CostEstimate(
            flops=4 * heads * TOK * keys * HD,
            bytes_accessed=3 << 20,
            transcendentals=heads * TOK * keys,
        ),
    )(*ins)


def project_kernel(place_ref, a_ref, *refs):
    weights, out_ref = refs[:18], refs[18]
    a = a_ref[...]
    for i in range(16):
        both = jnp.concatenate(pair_of(weights, i, W_ROWS), axis=1)
        r = jnp.dot(a, both, preferred_element_type=f32).astype(bf16)
        target = place_ref[i % 8]
        core = place_ref[8] if i < 8 else 1 - place_ref[8]
        yh = place_ref[9]
        for k in range(2):
            block = (yh if k == 0 else 1 - yh) * 2 + core
            out_ref[target, :, pl.ds(pl.multiple_of(block * 128, 128), 128)] = r[
                :, k * 128 : (k + 1) * 128
            ]


def project(place, heads_out, pieces):
    return pl.pallas_call(
        project_kernel,
        out_shape=jax.ShapeDtypeStruct((N_EXPERT, TOK, WIDTH), bf16),
        in_specs=[pl.BlockSpec(memory_space=pltpu.SMEM)]
        + [pl.BlockSpec(memory_space=pltpu.VMEM)] * 19,
        out_specs=pl.BlockSpec(memory_space=pltpu.VMEM),
        compiler_params=pltpu.CompilerParams(vmem_limit_bytes=20 << 20),
        cost_estimate=pl.CostEstimate(
            flops=2 * TOK * WIDTH * D, bytes_accessed=5 << 20, transcendentals=0
        ),
    )(place, heads_out, *pieces)


def experts_in(chunk):
    return tuple(x for x in range(2) if chunk[0] < (x + 1) * CAP and chunk[1] > x * CAP)


def choose(chunk, axis, tile, values):
    if len(values) == 1:
        return values[0]
    rows = lax.broadcasted_iota(jnp.int32, values[0].shape, axis) + pl.program_id(0) * tile
    second = rows % (chunk[1] - chunk[0]) >= CAP - chunk[0]
    return jnp.where(second, values[1], values[0])


def up_kernel(chunk, tile, count, carried, final, source_ref, *refs):
    refs = list(refs)
    before = [refs.pop(0) for _ in range(2)] if carried else None
    pieces = [refs.pop(0) for _ in range(count)]
    gates = [refs.pop(0) for _ in range(count)]
    ups = [refs.pop(0) for _ in range(count)]
    inverses = [refs.pop(0) for _ in range(count)]
    contract = (((1,), (1,)), ((), ()))
    experts = experts_in(chunk)
    total, squares = None, None
    for i in range(count):
        rows = pieces[i][...]
        weights = jnp.concatenate([ref[x] for ref in (gates[i], ups[i]) for x in experts], axis=0)
        term = lax.dot_general(weights, rows, contract, preferred_element_type=f32)
        total = term if total is None else total + term
        plain = rows.astype(f32) * inverses[i][...]
        squares = plain * plain if squares is None else squares + plain * plain
    ones = jnp.ones((16, WIDTH), bf16)
    high = squares.astype(bf16)
    low = (squares - high.astype(f32)).astype(bf16)
    square = lax.dot_general(ones, high, contract, preferred_element_type=f32)
    square = square + lax.dot_general(ones, low, contract, preferred_element_type=f32)
    parts = [total[k * HID_DEV : (k + 1) * HID_DEV] for k in range(2 * len(experts))]
    gate = choose(chunk, 1, tile, parts[: len(experts)])
    up = choose(chunk, 1, tile, parts[len(experts) :])
    if carried:
        gate = gate + before[0][:HID_DEV]
        up = up + before[0][HID_DEV:]
        square = square + before[1][...]
    if not final:
        refs[0][:HID_DEV] = gate
        refs[0][HID_DEV:] = up
        refs[1][...] = square
        return
    scale = lax.rsqrt(square / D + norm_epsilon)[:1]
    gate, up = gate * scale, up * scale
    refs[0][...] = (gate / (1.0 + jnp.exp(-gate)) * up).astype(bf16)


def up_project(chunk, source, inverse, gate_weight, up_weight, pieces, before, final, tile=256):
    rows = pieces[0].shape[0]
    count = len(pieces)

    def weight(i):
        return pl.BlockSpec((2, HID_DEV, WIDTH), lambda r, at: (0, 0, at[i]))

    def gain(i):
        return pl.BlockSpec((1, WIDTH), lambda r, at: (0, at[i]))

    sums = [
        pl.BlockSpec((2 * HID_DEV, tile), lambda r, at: (0, r)),
        pl.BlockSpec((16, tile), lambda r, at: (0, r)),
    ]
    act = pl.BlockSpec((HID_DEV, tile), lambda r, at: (0, r))
    return pl.pallas_call(
        functools.partial(up_kernel, chunk, tile, count, before is not None, final),
        out_shape=jax.ShapeDtypeStruct((HID_DEV, rows), bf16)
        if final
        else (
            jax.ShapeDtypeStruct((2 * HID_DEV, rows), f32),
            jax.ShapeDtypeStruct((16, rows), f32),
        ),
        grid_spec=pltpu.PrefetchScalarGridSpec(
            num_scalar_prefetch=1,
            grid=(rows // tile,),
            in_specs=(sums if before is not None else [])
            + [pl.BlockSpec((tile, WIDTH), lambda r, at: (r, 0))] * count
            + [weight(i) for i in range(count)] * 2
            + [gain(i) for i in range(count)],
            out_specs=act if final else tuple(sums),
        ),
        compiler_params=pltpu.CompilerParams(vmem_limit_bytes=28 << 20),
        cost_estimate=pl.CostEstimate(
            flops=4 * len(experts_in(chunk)) * rows * count * WIDTH * HID_DEV,
            bytes_accessed=count * (2 << 20),
            transcendentals=rows * HID_DEV,
        ),
    )(
        source,
        *(before or ()),
        *pieces,
        *([gate_weight] * count),
        *([up_weight] * count),
        *([inverse] * count),
    )


def down_kernel(chunk, tile, count, carried, final, *refs):
    refs = list(refs)
    before = refs.pop(0) if carried else None
    acts, weights, out_ref = refs[:count], refs[count : 2 * count], refs[2 * count]
    contract = (((0,), (0,)), ((), ()))
    act = jnp.concatenate([ref[...] for ref in acts], axis=0)
    outs = []
    for x in experts_in(chunk):
        weight = jnp.concatenate([ref[x] for ref in weights], axis=0)
        outs.append(lax.dot_general(act, weight, contract, preferred_element_type=f32))
    out = choose(chunk, 0, tile, outs)
    if carried:
        out = out + before[...]
    out_ref[...] = out.astype(out_ref.dtype)


def down_project(chunk, acts, weights, before, final, tile=256):
    rows = acts[0].shape[1]
    count = len(acts)
    out = pl.BlockSpec((tile, WIDTH), lambda r: (r, 0))
    return pl.pallas_call(
        functools.partial(down_kernel, chunk, tile, count, before is not None, final),
        out_shape=jax.ShapeDtypeStruct((rows, WIDTH), bf16 if final else f32),
        grid=(rows // tile,),
        in_specs=([out] if before is not None else [])
        + [pl.BlockSpec((HID_DEV, tile), lambda r: (0, r))] * count
        + [pl.BlockSpec((2, HID_DEV, WIDTH), lambda r: (0, 0, 0))] * count,
        out_specs=out,
        compiler_params=pltpu.CompilerParams(vmem_limit_bytes=20 << 20),
        cost_estimate=pl.CostEstimate(
            flops=2 * len(experts_in(chunk)) * rows * count * HID_DEV * WIDTH,
            bytes_accessed=count * (1 << 20) + (3 << 20),
            transcendentals=0,
        ),
    )(*([before] if before is not None else []), *acts, *weights)


def local(
    queries,
    key_rows,
    value_rows,
    span_order,
    residual,
    norm_gain,
    out_weight,
    gate_weight,
    up_weight,
    down_weight,
    routes,
    route_weights,
):
    context = lax.axis_index("context")
    expert = lax.axis_index("expert")
    z, yh, core = context // 4, (context // 2) % 2, context % 2
    x, yl = expert // 2, expert % 2

    column = (expert * (QH // N_EXPERT) // (QH // KVH)) * HD
    share = jnp.concatenate(
        [
            out_weight,
            lax.dynamic_slice_in_dim(key_rows, column, HD, 1),
            lax.dynamic_slice_in_dim(value_rows, column, HD, 1),
        ],
        axis=0,
    )
    steps = jnp.array(RING, jnp.int32)
    ring_z = (z + steps) % NZ
    both = jnp.arange(2, dtype=jnp.int32)
    owner = (
        (ring_z[None, :, None] * NY + (yh + both)[None, None, :] % NY) * NCORE
        + ((core + both) % NCORE)[:, None, None]
    ).reshape(N_CONTEXT)
    span_ids = owner[:, None] * 2 + both
    ids = jnp.arange(span_order.shape[0], dtype=jnp.int32)
    spans = jnp.sum(jnp.where(span_ids[:, :, None] == ids, span_order, 0), axis=2)
    inner = jnp.arange(SPAN, dtype=jnp.int32)
    kpos = (spans[:, :, None] * SPAN + inner).reshape(1, N_CONTEXT * TOK)
    pair = lax.dynamic_slice_in_dim(span_order, context * 2, 2)
    qpos = (pair[:, None] * SPAN + inner).reshape(TOK, 1)
    qpos = jnp.concatenate([qpos] * (queries.shape[1] // HD), axis=0)

    expert_ids = jnp.arange(EXPERTS, dtype=jnp.int32)
    matches = routes[:, :, None] == expert_ids
    member = jnp.any(matches, axis=1)
    shares = route_weights / jnp.sum(route_weights, axis=1, keepdims=True)
    share_of = jnp.sum(jnp.where(matches, shares[:, :, None], 0.0), axis=1)
    token_ids = jnp.arange(TOK, dtype=jnp.int32)
    earlier = (token_ids[None, :] < token_ids[:, None]).astype(bf16)
    before = jnp.dot(earlier, member.astype(bf16), preferred_element_type=f32)
    code = jnp.where(member, before, -1.0).astype(bf16)
    share_high = share_of.astype(bf16)
    share_low = (share_of - share_high.astype(f32)).astype(bf16)
    source = jnp.stack(
        [((x + dx) % NX) * NYL + (yl + dl) % NYL for dx, dl in PIECES]
    ).astype(jnp.int32)
    last = (((1,), (1,)), ((), ()))
    sends, returns = [], []
    for first, end in CHUNKS:
        per_block = end - first
        row_ids = jnp.arange(N_CONTEXT * per_block, dtype=jnp.int32)
        place_ids = first + row_ids % per_block
        row_expert = row_ids // per_block * 2 + place_ids // CAP
        spread = (row_expert[:, None] == expert_ids).astype(bf16)
        slot_of = (place_ids % CAP).astype(f32)
        coded = lax.dot_general(spread, code, last, preferred_element_type=f32)
        sends.append((coded == slot_of[:, None]).astype(bf16))
        coded = lax.dot_general(code, spread, last, preferred_element_type=f32)
        taken = coded == slot_of[None, :]
        returns.append(
            [
                jnp.where(
                    taken, lax.dot_general(part, spread, last, preferred_element_type=f32), 0.0
                ).astype(bf16)
                for part in (share_high, share_low)
            ]
        )


    down_cuts = []
    for dx, dl in PIECES:
        target = ((x - dx) % NX) * NYL + (yl + dl) % NYL
        down_cuts.append(lax.dynamic_slice_in_dim(down_weight, target * WIDTH, WIDTH, 2))

    def keys_of(table, which):
        cuts = [table[:, begin[i] : begin[i] + (256 if i % 9 < 7 else 128)] for i in which]
        return jnp.concatenate(cuts, axis=1)

    begin = [256 * i for i in range(8)] + [1920]
    begin = begin + [2048 + v for v in begin]
    sets = (
        (0, 1, 2, 3, 4, 9, 10, 11),
        (5, 6, 12, 13),
        (7, 8, 14, 15, 16, 17),
    )
    parts = []

    def attend(step):
        def run(mine, other):
            pieces = [(other if i > 8 else mine)[i % 9] for i in sets[step]]
            before = parts[-1] if parts else None
            part = attention(queries, qpos, keys_of(kpos, sets[step]), pieces, before, step == 2)
            parts.append(part)
            return part

        return run

    def down_from(i):
        return shift(down_cuts[i], dx=-PIECES[i][0])

    def relayed(i):
        return shift(down_cuts[i], dl=1)

    start = jnp.stack([share, shift(share, dy=1)])
    start, down_cuts = lax.optimization_barrier((start, down_cuts))
    ring_pieces, made = context_ring(
        start,
        [
            lambda mine, other: [down_from(1), relayed(3), down_cuts],
            lambda mine, other: [down_from(2), relayed(5), sends, returns],
            lambda mine, other: [down_from(4), relayed(6), attend(0)(mine, other)],
            lambda mine, other: [relayed(7), attend(1)(mine, other)],
        ],
    )
    xp_down, y_down, down_cuts = made[0]
    xm_down, xmy_down, sends, returns = made[1]
    two_down, xpy_down, _ = made[2]
    far_down, parts[-1] = made[3]
    heads_out = attend(2)(ring_pieces[:9], ring_pieces[9:])
    place = jnp.concatenate([ring_z, core[None], yh[None]]).astype(jnp.int32)
    terms = project(place, heads_out, ring_pieces)
    parts = lax.all_to_all(terms, "expert", 0, 0, tiled=True)
    state = residual.astype(f32) + jnp.sum(parts.astype(f32), axis=0)

    gain = lax.dynamic_slice_in_dim(norm_gain, expert * WIDTH, WIDTH)
    scaled = (state * gain).astype(bf16)
    inverse = (1.0 / norm_gain)[None]

    received = []
    for table in sends:
        rows = jnp.dot(table, scaled, preferred_element_type=f32).astype(bf16)
        if received:
            rows, received[-1] = lax.optimization_barrier((rows, received[-1]))
        received.append(lax.all_to_all(rows, "context", 0, 0, tiled=True))
    down_pieces = [down_cuts[0], xp_down, xm_down, y_down, two_down]
    down_pieces += [
        shift(xmy_down, dx=1),
        shift(xpy_down, dx=-1),
        shift(far_down, dx=2),
    ]
    received[0], down_pieces = lax.optimization_barrier((received[0], down_pieces))
    mixture = None
    for chunk, rows, weights in zip(CHUNKS, received, returns):

        def up(group, at, carry):
            to = at + len(group)
            return up_project(
                chunk, source[at:to], inverse, gate_weight, up_weight, group, carry, to == 8
            )

        def down(group, at, carry):
            to = at + len(group)
            return down_project(chunk, group, down_pieces[at:to], carry, to == 8)

        out = expert_stages(expert_stages(rows, up), down)
        returned = lax.all_to_all(out, "context", 0, 0, tiled=True)
        for part in weights:
            term = jnp.dot(part, returned, preferred_element_type=f32)
            mixture = term if mixture is None else mixture + term
    return (state.astype(bf16), (state + mixture).astype(bf16))


def solution(mesh):
    return jax.shard_map(
        local,
        mesh=mesh,
        in_specs=(
            P("context", "expert"),
            P("context", None),
            P("context", None),
            P(),
            P("context", "expert"),
            P(),
            P("expert", "context"),
            P("context", "expert", None),
            P("context", "expert", None),
            P("context", "expert", None),
            P("context", None),
            P("context", None),
        ),
        out_specs=(P("context", "expert"), P("context", "expert")),
        check_vma=False,
    )
```

```python
import functools

import jax
import jax.numpy as jnp
from jax import lax
from jax.experimental import pallas as pl
from jax.experimental.pallas import tpu as pltpu
from jax.sharding import PartitionSpec as P

D = 4096
HD = 128
QH = 32
KVH = 4
TOPK = 8
EXPERTS = 64
CAP = 20
SPAN = 64
NZ, NY, NCORE, NX, NYL = 8, 2, 2, 4, 2
N_CONTEXT = NZ * NY * NCORE
N_EXPERT = NX * NYL
CHUNKS = ((0, 40),)
WIDTH = D // N_EXPERT
HID_DEV = 192
TOK = 128

masked_score = -1e30
norm_epsilon = 1e-06
AXES = ("context", "expert")
f32 = jnp.float32
bf16 = jnp.bfloat16

RING = (0, -1, 1, -2, 2, -3, 3, 4)
PIECES = ((0, 0), (1, 0), (-1, 0), (0, 1), (2, 0), (-1, 1), (1, 1), (2, 1))


def flat_index(z, yh, core, x, yl):
    context = ((z % NZ) * NY + yh % NY) * NCORE + core % NCORE
    return context * N_EXPERT + (x % NX) * NYL + yl % NYL


@functools.lru_cache(None)
def pairs(dz, dy, dc, dx, dl):
    out = []
    for z in range(NZ):
        for yh in range(NY):
            for core in range(NCORE):
                for x in range(NX):
                    for yl in range(NYL):
                        out.append(
                            (
                                flat_index(z, yh, core, x, yl),
                                flat_index(z + dz, yh + dy, core + dc, x + dx, yl + dl),
                            )
                        )
    return tuple(out)


def shift(value, dz=0, dy=0, dc=0, dx=0, dl=0):
    return lax.ppermute(value, AXES, pairs(dz, dy, dc, dx, dl))


def context_ring(start, beside):
    up = down = start
    mine, other, made = [start], [], []
    waiting = [start]
    for step in range(3):
        cores = [shift(v, dc=1) for v in waiting]
        up, down = shift(up, dz=1), shift(down, dz=-1)
        up, down, cores, more = lax.optimization_barrier(
            (up, down, cores, beside[step](mine, other))
        )
        mine += [up, down]
        other += cores
        made.append(more)
        waiting = [up, down]
    cores = [shift(v, dc=1) for v in waiting]
    ends = [shift(up[0], dz=1), shift(down[1], dz=-1)]
    ends, cores, more = lax.optimization_barrier((ends, cores, beside[3](mine, other)))
    made.append(more)
    other += cores + [shift(v, dc=1) for v in ends]
    return mine + ends + other, made


def pair_of(refs, i, rows):
    half, step = divmod(i, 8)
    refs = refs[9 * half : 9 * half + 9]
    if step < 7:
        return refs[step][0, rows], refs[step][1, rows]
    return refs[7][rows], refs[8][rows]


def thirds_kernel(*refs):
    for source, target in zip(refs[:3], refs[3:]):
        target[...] = source[...]


def thirds(*arrays):
    rows, columns = arrays[0].shape
    part = -(-rows // 3 // 16) * 16
    specs = [
        pl.BlockSpec((part, columns), functools.partial(lambda k, r: (k, 0), k)) for k in range(3)
    ]
    return pl.pallas_call(
        thirds_kernel,
        out_shape=(jax.ShapeDtypeStruct((part, columns), arrays[0].dtype),) * 3,
        grid=(1,),
        in_specs=specs,
        out_specs=(pl.BlockSpec((part, columns), lambda r: (0, 0)),) * 3,
        compiler_params=pltpu.CompilerParams(vmem_limit_bytes=24 << 20),
        cost_estimate=pl.CostEstimate(
            flops=0, bytes_accessed=2 * rows * columns * 2, transcendentals=0
        ),
    )(*arrays)


def expert_stages(v, consume):
    first = (shift(v, dx=-1), shift(v, dx=1), shift(v, dl=1))
    carry = consume([v], 0, None)
    (xp, xm, yy), carry = lax.optimization_barrier((first, carry))
    second = (shift(xp, dx=-1), shift(yy, dx=1), shift(xp, dl=1))
    carry = consume([xp, xm, yy], 1, carry)
    (x2, xmy, xpy), carry = lax.optimization_barrier((second, carry))
    cut = thirds(x2, xmy, xpy)
    last = (shift(cut[0], dl=1), shift(cut[1], dx=1), shift(cut[2], dx=-1))
    carry = consume([x2, xmy, xpy], 4, carry)
    last, carry = lax.optimization_barrier((last, carry))
    return consume([jnp.concatenate(last, axis=0)[: v.shape[0]]], 7, carry)


W_ROWS = slice(0, 512)
K_ROWS = slice(512, 640)
V_ROWS = slice(640, 768)


def attention_kernel(count, carried, final, q_ref, qpos_ref, kpos_ref, *refs):
    refs = list(refs)
    before = [refs.pop(0) for _ in range(3)] if carried else None
    pieces = [refs.pop(0) for _ in range(count)]
    scores = refs.pop()
    heads = q_ref.shape[1] // HD
    q = jnp.concatenate([q_ref[:, h * HD : (h + 1) * HD] for h in range(heads)], axis=0)
    qpos = qpos_ref[...]
    top = None

    def rows_of(i, rows):
        ref = pieces[i]
        if len(ref.shape) == 2:
            return ref[rows]
        return jnp.concatenate([ref[0, rows], ref[1, rows]], axis=0)

    spans = []
    at = 0
    for i in range(count):
        keys = rows_of(i, K_ROWS)
        span = slice(at, at + keys.shape[0])
        spans.append(span)
        at = span.stop
        s = lax.dot_general(q, keys, (((1,), (1,)), ((), ())), preferred_element_type=f32)
        s = jnp.where(kpos_ref[:, span] <= qpos, s * (HD**-0.5), masked_score)
        scores[:, span] = s
        m = jnp.maximum(s[:, :HD], s[:, HD:]) if s.shape[1] > HD else s
        top = m if top is None else jnp.maximum(top, m)
    top = jnp.max(top, axis=1, keepdims=True)
    if carried:
        top = jnp.maximum(top, before[0][:, :1])
    total = None
    acc = None
    for i, span in enumerate(spans):
        p = jnp.exp(scores[:, span] - top)
        t = p[:, :HD] + p[:, HD:] if p.shape[1] > HD else p
        total = t if total is None else total + t
        term = jnp.dot(p.astype(bf16), rows_of(i, V_ROWS), preferred_element_type=f32)
        acc = term if acc is None else acc + term
    if carried:
        factor = jnp.exp(before[0][:, :1] - top)
        total = total + before[1][...] * factor
        acc = acc + before[2][...] * factor
    if not final:
        refs[0][...] = jnp.broadcast_to(top, (heads * TOK, HD))
        refs[1][...] = total
        refs[2][...] = acc
        return
    out = (acc / jnp.sum(total, axis=1, keepdims=True)).astype(bf16)
    for h in range(heads):
        refs[0][:, h * HD : (h + 1) * HD] = out[h * TOK : (h + 1) * TOK]


def attention(queries, qpos, kpos, pieces, before, final):
    heads = queries.shape[1] // HD
    keys = kpos.shape[1]
    part = jax.ShapeDtypeStruct((heads * TOK, HD), f32)
    ins = (queries, qpos, kpos, *(before or ()), *pieces)
    return pl.pallas_call(
        functools.partial(attention_kernel, len(pieces), before is not None, final),
        out_shape=jax.ShapeDtypeStruct(queries.shape, bf16) if final else (part, part, part),
        in_specs=[pl.BlockSpec(memory_space=pltpu.VMEM)] * len(ins),
        out_specs=pl.BlockSpec(memory_space=pltpu.VMEM)
        if final
        else (pl.BlockSpec(memory_space=pltpu.VMEM),) * 3,
        scratch_shapes=[pltpu.VMEM((heads * TOK, keys), f32)],
        compiler_params=pltpu.CompilerParams(vmem_limit_bytes=20 << 20),
        cost_estimate=pl.CostEstimate(
            flops=4 * heads * TOK * keys * HD,
            bytes_accessed=3 << 20,
            transcendentals=heads * TOK * keys,
        ),
    )(*ins)


def project_kernel(place_ref, a_ref, *refs):
    weights, out_ref = refs[:18], refs[18]
    a = a_ref[...]
    for i in range(16):
        both = jnp.concatenate(pair_of(weights, i, W_ROWS), axis=1)
        r = jnp.dot(a, both, preferred_element_type=f32).astype(bf16)
        target = place_ref[i % 8]
        core = place_ref[8] if i < 8 else 1 - place_ref[8]
        yh = place_ref[9]
        for k in range(2):
            block = (yh if k == 0 else 1 - yh) * 2 + core
            out_ref[target, :, pl.ds(pl.multiple_of(block * 128, 128), 128)] = r[
                :, k * 128 : (k + 1) * 128
            ]


def project(place, heads_out, pieces):
    return pl.pallas_call(
        project_kernel,
        out_shape=jax.ShapeDtypeStruct((N_EXPERT, TOK, WIDTH), bf16),
        in_specs=[pl.BlockSpec(memory_space=pltpu.SMEM)]
        + [pl.BlockSpec(memory_space=pltpu.VMEM)] * 19,
        out_specs=pl.BlockSpec(memory_space=pltpu.VMEM),
        compiler_params=pltpu.CompilerParams(vmem_limit_bytes=20 << 20),
        cost_estimate=pl.CostEstimate(
            flops=2 * TOK * WIDTH * D, bytes_accessed=5 << 20, transcendentals=0
        ),
    )(place, heads_out, *pieces)


def experts_in(chunk):
    return tuple(x for x in range(2) if chunk[0] < (x + 1) * CAP and chunk[1] > x * CAP)


def choose(chunk, axis, tile, values):
    if len(values) == 1:
        return values[0]
    rows = lax.broadcasted_iota(jnp.int32, values[0].shape, axis) + pl.program_id(0) * tile
    second = rows % (chunk[1] - chunk[0]) >= CAP - chunk[0]
    return jnp.where(second, values[1], values[0])


def up_kernel(chunk, tile, count, carried, final, source_ref, *refs):
    refs = list(refs)
    before = [refs.pop(0) for _ in range(2)] if carried else None
    pieces = [refs.pop(0) for _ in range(count)]
    gates = [refs.pop(0) for _ in range(count)]
    ups = [refs.pop(0) for _ in range(count)]
    inverses = [refs.pop(0) for _ in range(count)]
    contract = (((1,), (1,)), ((), ()))
    experts = experts_in(chunk)
    total, squares = None, None
    for i in range(count):
        rows = pieces[i][...]
        weights = jnp.concatenate([ref[x] for ref in (gates[i], ups[i]) for x in experts], axis=0)
        term = lax.dot_general(weights, rows, contract, preferred_element_type=f32)
        total = term if total is None else total + term
        plain = rows.astype(f32) * inverses[i][...]
        squares = plain * plain if squares is None else squares + plain * plain
    ones = jnp.ones((16, WIDTH), bf16)
    high = squares.astype(bf16)
    low = (squares - high.astype(f32)).astype(bf16)
    square = lax.dot_general(ones, high, contract, preferred_element_type=f32)
    square = square + lax.dot_general(ones, low, contract, preferred_element_type=f32)
    parts = [total[k * HID_DEV : (k + 1) * HID_DEV] for k in range(2 * len(experts))]
    gate = choose(chunk, 1, tile, parts[: len(experts)])
    up = choose(chunk, 1, tile, parts[len(experts) :])
    if carried:
        gate = gate + before[0][:HID_DEV]
        up = up + before[0][HID_DEV:]
        square = square + before[1][...]
    if not final:
        refs[0][:HID_DEV] = gate
        refs[0][HID_DEV:] = up
        refs[1][...] = square
        return
    scale = lax.rsqrt(square / D + norm_epsilon)[:1]
    gate, up = gate * scale, up * scale
    refs[0][...] = (gate / (1.0 + jnp.exp(-gate)) * up).astype(bf16)


def up_project(chunk, source, inverse, gate_weight, up_weight, pieces, before, final, tile=256):
    rows = pieces[0].shape[0]
    count = len(pieces)

    def weight(i):
        return pl.BlockSpec((2, HID_DEV, WIDTH), lambda r, at: (0, 0, at[i]))

    def gain(i):
        return pl.BlockSpec((1, WIDTH), lambda r, at: (0, at[i]))

    sums = [
        pl.BlockSpec((2 * HID_DEV, tile), lambda r, at: (0, r)),
        pl.BlockSpec((16, tile), lambda r, at: (0, r)),
    ]
    act = pl.BlockSpec((HID_DEV, tile), lambda r, at: (0, r))
    return pl.pallas_call(
        functools.partial(up_kernel, chunk, tile, count, before is not None, final),
        out_shape=jax.ShapeDtypeStruct((HID_DEV, rows), bf16)
        if final
        else (
            jax.ShapeDtypeStruct((2 * HID_DEV, rows), f32),
            jax.ShapeDtypeStruct((16, rows), f32),
        ),
        grid_spec=pltpu.PrefetchScalarGridSpec(
            num_scalar_prefetch=1,
            grid=(rows // tile,),
            in_specs=(sums if before is not None else [])
            + [pl.BlockSpec((tile, WIDTH), lambda r, at: (r, 0))] * count
            + [weight(i) for i in range(count)] * 2
            + [gain(i) for i in range(count)],
            out_specs=act if final else tuple(sums),
        ),
        compiler_params=pltpu.CompilerParams(vmem_limit_bytes=28 << 20),
        cost_estimate=pl.CostEstimate(
            flops=4 * len(experts_in(chunk)) * rows * count * WIDTH * HID_DEV,
            bytes_accessed=count * (2 << 20),
            transcendentals=rows * HID_DEV,
        ),
    )(
        source,
        *(before or ()),
        *pieces,
        *([gate_weight] * count),
        *([up_weight] * count),
        *([inverse] * count),
    )


def down_kernel(chunk, tile, count, carried, final, *refs):
    refs = list(refs)
    before = refs.pop(0) if carried else None
    acts, weights, out_ref = refs[:count], refs[count : 2 * count], refs[2 * count]
    contract = (((0,), (0,)), ((), ()))
    act = jnp.concatenate([ref[...] for ref in acts], axis=0)
    outs = []
    for x in experts_in(chunk):
        weight = jnp.concatenate([ref[x] for ref in weights], axis=0)
        outs.append(lax.dot_general(act, weight, contract, preferred_element_type=f32))
    out = choose(chunk, 0, tile, outs)
    if carried:
        out = out + before[...]
    out_ref[...] = out.astype(out_ref.dtype)


def down_project(chunk, acts, weights, before, final, tile=256):
    rows = acts[0].shape[1]
    count = len(acts)
    out = pl.BlockSpec((tile, WIDTH), lambda r: (r, 0))
    return pl.pallas_call(
        functools.partial(down_kernel, chunk, tile, count, before is not None, final),
        out_shape=jax.ShapeDtypeStruct((rows, WIDTH), bf16 if final else f32),
        grid=(rows // tile,),
        in_specs=([out] if before is not None else [])
        + [pl.BlockSpec((HID_DEV, tile), lambda r: (0, r))] * count
        + [pl.BlockSpec((2, HID_DEV, WIDTH), lambda r: (0, 0, 0))] * count,
        out_specs=out,
        compiler_params=pltpu.CompilerParams(vmem_limit_bytes=20 << 20),
        cost_estimate=pl.CostEstimate(
            flops=2 * len(experts_in(chunk)) * rows * count * HID_DEV * WIDTH,
            bytes_accessed=count * (1 << 20) + (3 << 20),
            transcendentals=0,
        ),
    )(*([before] if before is not None else []), *acts, *weights)


def local(
    queries,
    key_rows,
    value_rows,
    span_order,
    residual,
    norm_gain,
    out_weight,
    gate_weight,
    up_weight,
    down_weight,
    routes,
    route_weights,
):
    context = lax.axis_index("context")
    expert = lax.axis_index("expert")
    z, yh, core = context // 4, (context // 2) % 2, context % 2
    x, yl = expert // 2, expert % 2

    column = (expert * (QH // N_EXPERT) // (QH // KVH)) * HD
    share = jnp.concatenate(
        [
            out_weight,
            lax.dynamic_slice_in_dim(key_rows, column, HD, 1),
            lax.dynamic_slice_in_dim(value_rows, column, HD, 1),
        ],
        axis=0,
    )
    steps = jnp.array(RING, jnp.int32)
    ring_z = (z + steps) % NZ
    both = jnp.arange(2, dtype=jnp.int32)
    owner = (
        (ring_z[None, :, None] * NY + (yh + both)[None, None, :] % NY) * NCORE
        + ((core + both) % NCORE)[:, None, None]
    ).reshape(N_CONTEXT)
    span_ids = owner[:, None] * 2 + both
    ids = jnp.arange(span_order.shape[0], dtype=jnp.int32)
    spans = jnp.sum(jnp.where(span_ids[:, :, None] == ids, span_order, 0), axis=2)
    inner = jnp.arange(SPAN, dtype=jnp.int32)
    kpos = (spans[:, :, None] * SPAN + inner).reshape(1, N_CONTEXT * TOK)
    pair = lax.dynamic_slice_in_dim(span_order, context * 2, 2)
    qpos = (pair[:, None] * SPAN + inner).reshape(TOK, 1)
    qpos = jnp.concatenate([qpos] * (queries.shape[1] // HD), axis=0)

    expert_ids = jnp.arange(EXPERTS, dtype=jnp.int32)
    matches = routes[:, :, None] == expert_ids
    member = jnp.any(matches, axis=1)
    shares = route_weights / jnp.sum(route_weights, axis=1, keepdims=True)
    share_of = jnp.sum(jnp.where(matches, shares[:, :, None], 0.0), axis=1)
    token_ids = jnp.arange(TOK, dtype=jnp.int32)
    earlier = (token_ids[None, :] < token_ids[:, None]).astype(bf16)
    before = jnp.dot(earlier, member.astype(bf16), preferred_element_type=f32)
    code = jnp.where(member, before, -1.0).astype(bf16)
    share_high = share_of.astype(bf16)
    share_low = (share_of - share_high.astype(f32)).astype(bf16)
    source = jnp.stack(
        [((x + dx) % NX) * NYL + (yl + dl) % NYL for dx, dl in PIECES]
    ).astype(jnp.int32)
    last = (((1,), (1,)), ((), ()))
    sends, returns = [], []
    for first, end in CHUNKS:
        per_block = end - first
        row_ids = jnp.arange(N_CONTEXT * per_block, dtype=jnp.int32)
        place_ids = first + row_ids % per_block
        row_expert = row_ids // per_block * 2 + place_ids // CAP
        spread = (row_expert[:, None] == expert_ids).astype(bf16)
        slot_of = (place_ids % CAP).astype(f32)
        coded = lax.dot_general(spread, code, last, preferred_element_type=f32)
        sends.append((coded == slot_of[:, None]).astype(bf16))
        coded = lax.dot_general(code, spread, last, preferred_element_type=f32)
        taken = coded == slot_of[None, :]
        returns.append(
            [
                jnp.where(
                    taken, lax.dot_general(part, spread, last, preferred_element_type=f32), 0.0
                ).astype(bf16)
                for part in (share_high, share_low)
            ]
        )


    def keys_of(table, which):
        cuts = [table[:, begin[i] : begin[i] + (256 if i % 9 < 7 else 128)] for i in which]
        return jnp.concatenate(cuts, axis=1)

    begin = [256 * i for i in range(8)] + [1920]
    begin = begin + [2048 + v for v in begin]
    sets = (
        (0, 1, 2, 3, 4, 9, 10, 11),
        (5, 6, 12, 13),
        (7, 8, 14, 15, 16, 17),
    )
    parts = []

    def attend(step):
        def run(mine, other):
            pieces = [(other if i > 8 else mine)[i % 9] for i in sets[step]]
            before = parts[-1] if parts else None
            part = attention(queries, qpos, keys_of(kpos, sets[step]), pieces, before, step == 2)
            parts.append(part)
            return part

        return run

    def down_from(i):
        return shift(down_cuts[i], dx=-PIECES[i][0])

    def relayed(i):
        return shift(down_cuts[i], dl=1)

    start = jnp.stack([share, shift(share, dy=1)])
    start, down_source = lax.optimization_barrier((start, down_weight))
    down_cuts = []
    for dx, dl in PIECES:
        target = ((x - dx) % NX) * NYL + (yl + dl) % NYL
        down_cuts.append(lax.dynamic_slice_in_dim(down_source, target * WIDTH, WIDTH, 2))
    ring_pieces, made = context_ring(
        start,
        [
            lambda mine, other: [down_from(1), relayed(3), down_cuts],
            lambda mine, other: [down_from(2), relayed(5), sends, returns],
            lambda mine, other: [down_from(4), relayed(6), attend(0)(mine, other)],
            lambda mine, other: [relayed(7), attend(1)(mine, other)],
        ],
    )
    xp_down, y_down, down_cuts = made[0]
    xm_down, xmy_down, sends, returns = made[1]
    two_down, xpy_down, _ = made[2]
    far_down, parts[-1] = made[3]
    heads_out = attend(2)(ring_pieces[:9], ring_pieces[9:])
    place = jnp.concatenate([ring_z, core[None], yh[None]]).astype(jnp.int32)
    terms = project(place, heads_out, ring_pieces)
    parts = lax.all_to_all(terms, "expert", 0, 0, tiled=True)
    state = residual.astype(f32) + jnp.sum(parts.astype(f32), axis=0)

    gain = lax.dynamic_slice_in_dim(norm_gain, expert * WIDTH, WIDTH)
    scaled = (state * gain).astype(bf16)
    inverse = (1.0 / norm_gain)[None]

    received = []
    for table in sends:
        rows = jnp.dot(table, scaled, preferred_element_type=f32).astype(bf16)
        if received:
            rows, received[-1] = lax.optimization_barrier((rows, received[-1]))
        received.append(lax.all_to_all(rows, "context", 0, 0, tiled=True))
    down_pieces = [down_cuts[0], xp_down, xm_down, y_down, two_down]
    down_pieces += [
        shift(xmy_down, dx=1),
        shift(xpy_down, dx=-1),
        shift(far_down, dx=2),
    ]
    received[0], down_pieces = lax.optimization_barrier((received[0], down_pieces))
    mixture = None
    for chunk, rows, weights in zip(CHUNKS, received, returns):

        def up(group, at, carry):
            to = at + len(group)
            return up_project(
                chunk, source[at:to], inverse, gate_weight, up_weight, group, carry, to == 8
            )

        def down(group, at, carry):
            to = at + len(group)
            return down_project(chunk, group, down_pieces[at:to], carry, to == 8)

        out = expert_stages(expert_stages(rows, up), down)
        returned = lax.all_to_all(out, "context", 0, 0, tiled=True)
        for part in weights:
            term = jnp.dot(part, returned, preferred_element_type=f32)
            mixture = term if mixture is None else mixture + term
    return (state.astype(bf16), (state + mixture).astype(bf16))


def solution(mesh):
    return jax.shard_map(
        local,
        mesh=mesh,
        in_specs=(
            P("context", "expert"),
            P("context", None),
            P("context", None),
            P(),
            P("context", "expert"),
            P(),
            P("expert", "context"),
            P("context", "expert", None),
            P("context", "expert", None),
            P("context", "expert", None),
            P("context", None),
            P("context", None),
        ),
        out_specs=(P("context", "expert"), P("context", "expert")),
        check_vma=False,
    )
```
